256 devices in a mesh: row: 16 (over z, core), col: 16 (over x, y).
Axes of the slice: x: 4, y: 4, z: 8, core: 2. Of those that a mesh axis runs over, the one named last changes fastest.
Arguments:
- out_grad: bfloat16 [65536, 128], P(('row', 'col')), may hold values from -6 to 6
- relu_mask: bfloat16 [65536, 128], P(('row', 'col')), may hold values from 0 to 1, as said below
- saved_agg: bfloat16 [65536, 128], P(('row', 'col')), may hold values from -0.059814453 to 0.059814453
- weight: bfloat16 [128, 128], replicated, may hold values from -0.5 to 0.5
- tile_values: bfloat16 [16, 16, 320, 128, 128], P('row', 'col'), may hold values from 0 to 0.012084961
- tile_coords: int32 [16, 16, 320, 2], P('row', 'col'), may hold values from 0 to 31, as said below
- tile_count: int32 [16, 16], P('row', 'col'), may hold values from 80 to 320, as said below
Outputs:
- input_grad: bfloat16 [65536, 128], P(('col', 'row'))
- weight_grad: float32 [128, 128], replicated
The draws below stay inside these ranges and needn't reach their ends.
Inputs may be any that keep to these rules, and one draw needn't show every extreme that they name: `tile_coords`: within one block the live and dead slots name distinct tiles; tile rows are below 32, tile columns below 32. Slots at or past tile_count are ignored. `tile_count`: live slots of a block; some block is full in every draw. `relu_mask`: entries are 0 or 1.
All inputs are finite; a program needn't handle non-finite values.
Results may differ from the reference program's by a relative error of at most 0.0049.
Values may be sent and summed in bfloat16 or wider, within the bound.
A program may use at most 128 MiB of HBM per device.

```python
import jax
import jax.numpy as jnp
from jax import lax

FIN = 128
HID = 128
TILE = 128
NODES = 65536
RT = 32
CT = 32
CAP = 320
N_ROW = 16
N_COL = 16


def draw_relu_mask(key, part):
    key = jax.random.fold_in(key, 13)
    chosen = jax.random.bernoulli(key, 0.5, (NODES, HID))
    return chosen.astype(jnp.float32).astype(jnp.bfloat16)


def draw_tile_coords(key, part):
    key = jax.random.fold_in(key, 11)
    subkeys = jax.random.split(key, N_ROW * N_COL)
    ordering = jax.vmap(lambda single: jax.random.permutation(single, RT * CT)[:CAP])(subkeys)
    ordering = ordering.astype(jnp.int32)
    paired = jnp.stack([ordering // CT, ordering % CT], axis=-1)
    return paired.reshape(N_ROW, N_COL, CAP, 2).astype(jnp.int32)


def draw_tile_count(key, part):
    key = jax.random.fold_in(key, 12)
    first_key, second_key, third_key = jax.random.split(key, 3)
    span = CAP - CAP // 4 + 1
    first_draw = jax.random.randint(first_key, (N_ROW * N_COL,), 0, span)
    second_draw = jax.random.randint(second_key, (N_ROW * N_COL,), 0, span)
    counts_drawn = CAP // 4 + first_draw * second_draw // (span - 1)
    fullest = jax.random.randint(third_key, (), 0, N_ROW * N_COL)
    positions = jnp.arange(N_ROW * N_COL, dtype=jnp.int32)
    counts_drawn = jnp.where(positions == fullest, CAP, counts_drawn)
    return counts_drawn.reshape(N_ROW, N_COL).astype(jnp.int32)


def block_levels(rng, extent, cuts, smallest, largest):
    gain = 1.0
    for position, blocks in cuts:
        draws = jax.random.uniform(jax.random.fold_in(jax.random.fold_in(rng, 6), position), (blocks,), jnp.float32, smallest / len(cuts), largest / len(cuts))
        gain = gain * jnp.repeat(jnp.exp(draws), extent[position] // blocks).reshape((-1,) + (1,) * (len(extent) - 1 - position))
    return gain


def bell_draw(key, shape, scale, bound, cuts=(), kind=jnp.bfloat16):
    array = jax.random.normal(key, shape, jnp.float32) * scale
    if len(cuts) > 0:
        array = block_levels(key, shape, cuts, -0.22, 0.18) * array
    return jnp.clip(array, min=-bound, max=bound).astype(kind)


def setup_inputs(seed: int = 0) -> dict:
    splits = jax.random.split(jax.random.key(seed), 8)
    return {
        "out_grad": bell_draw(splits[0], (NODES, HID), 1.0, 6.0, ((0, 256),)),
        "relu_mask": draw_relu_mask(jax.random.fold_in(splits[7], 71), 0),
        "saved_agg": bell_draw(splits[2], (NODES, FIN), 0.01, 0.059814453, ((0, 256),)),
        "weight": bell_draw(splits[3], (FIN, HID), HID ** -0.5, 0.5),
        "tile_values": jnp.clip(0.012084961 * jax.random.uniform(splits[4], (N_ROW, N_COL, CAP, TILE, TILE), jnp.float32) ** block_levels(splits[4], (N_ROW, N_COL, CAP, TILE, TILE), ((0, 16), (1, 16)), -0.2, 0.2), 0.0, 0.012084961).astype(jnp.bfloat16),
        "tile_coords": draw_tile_coords(jax.random.fold_in(splits[7], 71), 0),
        "tile_count": draw_tile_count(jax.random.fold_in(splits[7], 71), 0),
    }


def reference(out_grad, relu_mask, saved_agg, weight, tile_values, tile_coords, tile_count):
    pre_grad = (out_grad.astype(jnp.float32) * relu_mask.astype(jnp.float32)).astype(jnp.bfloat16)
    weight_grad = jnp.dot(saved_agg.T, pre_grad, preferred_element_type=jnp.float32)
    agg_grad = jnp.dot(pre_grad, weight.T, preferred_element_type=jnp.float32).astype(jnp.bfloat16)
    panels = agg_grad.reshape(N_ROW, RT, TILE, FIN)
    live = (jnp.arange(CAP, dtype=jnp.int32)[None, None, :] < tile_count[:, :, None]).astype(jnp.float32)
    columns = jnp.arange(CT, dtype=jnp.int32)

    def one_block(total, inputs):
        values, coords, alive, panel = inputs
        gathered = panel[coords[..., 0]]
        products = jnp.einsum("jkab,jkaf->jkbf", values.astype(jnp.float32), gathered.astype(jnp.float32))
        selector = (coords[..., 1][:, :, None] == columns[None, None, :]).astype(jnp.float32) * alive[:, :, None]
        added = jnp.einsum("jkc,jkbf->jcbf", selector, products, precision=lax.Precision.HIGHEST)
        return total + added, None

    start = jnp.zeros((N_COL, CT, TILE, FIN), jnp.float32)
    total, unused = lax.scan(one_block, start, (tile_values, tile_coords, live, panels))
    input_grad = total.reshape(NODES, FIN).astype(jnp.bfloat16)
    return input_grad, weight_grad
```

```python
import functools

import jax
import jax.numpy as jnp
from jax import lax
from jax.experimental import pallas as pl
from jax.experimental.pallas import tpu as pltpu
from jax.sharding import PartitionSpec as P

MESH = pl.DeviceIdType.MESH
F32 = jnp.float32
BF16 = jnp.bfloat16

TILE = 128
SLOTS = 320
COLS = 32
HALF = 64
PAIRS = SLOTS // 2 + COLS // 2
LANES = 384
UNROLL = 8
CHUNKS = 4


def order_slots(coords, count):
    def total(condition, value, axis):
        return jnp.sum(jnp.where(condition, value, 0), axis=axis, keepdims=True)

    def iota(shape, axis):
        return lax.broadcasted_iota(jnp.int32, shape, axis)

    square = (SLOTS, SLOTS)
    down, across = iota(square, 0), iota(square, 1)
    live = iota((1, SLOTS), 1) < jnp.broadcast_to(count, (1, SLOTS))
    row = coords[0:1, :]
    key = jnp.where(live, coords[1:2, :], COLS)
    key_all = jnp.broadcast_to(key, square)
    key_down = total(down == across, key_all, 1)
    row_down = total(down == across, jnp.broadcast_to(row, square), 1)
    rank = total((key_down == key_all) & (across < down), 1, 1)

    member = key_down == iota((SLOTS, 128), 1)
    count_lane = total(member, 1, 0)
    count_down = total(jnp.broadcast_to(key, (COLS, SLOTS)) == iota((COLS, SLOTS), 0), 1, 1)
    padded_lane = (count_lane + 1) // 2 * 2
    padded_down = (count_down + 1) // 2 * 2
    low, high = iota((COLS, 128), 0), iota((COLS, 128), 1)
    start_lane = total(low < high, padded_down, 0)
    start_down = total(high < low, padded_lane, 1)

    place = jnp.where(key_down < COLS, total(member, start_lane, 1) + rank, -1)
    payload = iota((SLOTS, 1), 0) * 64 + row_down - COLS
    packed = COLS + total(place == iota((SLOTS, LANES), 1), payload, 0)

    pair = 2 * iota((COLS, LANES), 1)
    keep = 1 - total((start_down == pair) & (count_down > 0), 1, 0)
    last = jnp.where(count_lane > 0, (start_lane + padded_lane) // 2 - 1, PAIRS)
    return packed, keep, last


def kernel(
    out_grad, relu_mask, saved_agg, weight, tile_values, coords, count, input_grad, weight_grad,
    og, rm, sa, wt, tiles, xy, ct, meta_v, meta,
    agg0, agg1, run0, run1, xsend, xrecv, zsend, zrecv, own, term, areceived, breceived, creceived,
    load_sem, tile_sem, first_recv, second_recv, gather_send,
    xs_sem, xr_sem, zs_sem, zr_sem, w_send, w_recv,
):
    row, col = lax.axis_index("row"), lax.axis_index("col")
    z, core, x, y = row // 2, row % 2, col // 4, col % 4

    def at(xx, yy):
        return (row, xx % 4 * 4 + yy % 4)

    def up(d):
        return ((z + d) % 8 * 2 + core, col)

    partner = (z * 2 + 1 - core, col)
    plane = [(a, b) for a in range(4) for b in range(4) if a or b]

    barrier = pltpu.get_barrier_semaphore()
    for a, b in plane:
        pl.semaphore_signal(barrier, inc=1, device_id=at(x + a, y + b), device_id_type=MESH)
    for d in range(1, 8):
        pl.semaphore_signal(barrier, inc=1, device_id=up(d), device_id_type=MESH)
    pl.semaphore_signal(barrier, inc=1, device_id=partner, device_id_type=MESH)

    loads = [
        pltpu.make_async_copy(src, dst, load_sem.at[i])
        for i, (src, dst) in enumerate(
            ((out_grad, og), (relu_mask, rm), (weight, wt), (saved_agg, sa), (coords, xy), (count, ct))
        )
    ]
    for load in loads:
        load.start()
    step = SLOTS // CHUNKS
    tile_loads = [
        pltpu.make_async_copy(
            tile_values.at[0, 0, pl.ds(i * step, step)], tiles.at[pl.ds(i * step, step)], tile_sem.at[i]
        )
        for i in range(CHUNKS)
    ]
    for load in tile_loads:
        load.start()

    aggs, runs = (agg0, agg1), (run0, run1)
    for agg in aggs:
        agg[COLS] = jnp.zeros((HALF, TILE), BF16)
    for run in runs:
        run[PAIRS] = jnp.zeros((HALF, TILE), F32)

    for load in loads[:3]:
        load.wait()
    pre = (og[...].astype(F32) * rm[...].astype(F32)).astype(BF16)
    mine = lax.dot_general(wt[...], pre, (((1,), (1,)), ((), ())), preferred_element_type=F32).astype(BF16)
    for h in range(2):
        for e in range(2):
            aggs[h][2 * col + e] = mine[h * HALF : (h + 1) * HALF, e * TILE : (e + 1) * TILE]

    pl.semaphore_wait(barrier, len(plane) + 8)

    def toward(e, phase, d):
        return at(x + d, y) if (e + phase) % 2 == 0 else at(x, y + d)

    def piece(e, d):
        a, b = ((x - d) % 4, y) if e == 0 else (x, (y - d) % 4)
        return 2 * (a * 4 + b) + e

    def gather_copy(h, r, recv, target):
        block = aggs[h].at[r]
        return pltpu.make_async_remote_copy(
            src_ref=block, dst_ref=block, send_sem=gather_send.at[h], recv_sem=recv, device_id=target, device_id_type=MESH
        )

    def second(h, e, r):
        for d in (2, 1, 3):
            gather_copy(h, r, second_recv.at[h], toward(e, 1, d)).start()

    for h in range(2):
        for e in range(2):
            for d in (2, 1, 3):
                gather_copy(h, 2 * col + e, first_recv.at[h * 6 + e * 3 + d - 1], toward(e, 0, d)).start()
        for e in range(2):
            second(h, e, 2 * col + e)

    loads[3].wait()
    term[...] = lax.dot_general(sa[...], pre, (((0,), (0,)), ((), ())), preferred_element_type=F32)
    areceived[col] = term[pl.ds(pl.multiple_of(col * 8, 8), 8), :]
    for a, b in plane:
        target = (x + a) % 4 * 4 + (y + b) % 4
        pltpu.make_async_remote_copy(
            src_ref=term.at[pl.ds(pl.multiple_of(target * 8, 8), 8)], dst_ref=areceived.at[col],
            send_sem=w_send.at[0], recv_sem=w_recv.at[0], device_id=(row, target), device_id_type=MESH,
        ).start()

    loads[4].wait()
    loads[5].wait()
    packed, keep, last = order_slots(xy[...], ct[...])
    meta_v[...] = jnp.full((8, LANES), PAIRS, jnp.int32)
    meta_v[0:1, :] = packed
    meta_v[1:2, :] = keep
    meta_v[2:3, 0:128] = last
    to_scalar = pltpu.make_async_copy(meta_v, meta, load_sem.at[6])
    to_scalar.start()

    for h in range(2):
        for e in range(2):
            for d in range(1, 4):
                r = piece(e, d)
                gather_copy(h, r, first_recv.at[h * 6 + e * 3 + d - 1], toward(e, 0, d)).wait_recv()
                second(h, e, r)
    to_scalar.wait()
    for load in tile_loads:
        load.wait()

    def gathered(h):
        part = aggs[h].at[pl.ds(0, 24)]
        pltpu.make_async_copy(part, part, second_recv.at[h]).wait()

    def products(h):
        agg, run = aggs[h], runs[h]

        def body(t, total):
            for u in range(UNROLL):
                q = t * UNROLL + u
                a, b = meta[0, 2 * q], meta[0, 2 * q + 1]
                left = jnp.concatenate([agg[a & 63], agg[b & 63]], axis=1)
                right = jnp.concatenate([tiles[a >> 6], tiles[b >> 6]], axis=0)
                total = total * meta[1, q].astype(F32) + jnp.dot(left, right, preferred_element_type=F32)
                run[q] = total
            return total

        lax.fori_loop(0, PAIRS // UNROLL, body, jnp.zeros((HALF, TILE), F32))

    def swap(h):
        return pltpu.make_async_remote_copy(
            src_ref=xsend.at[h], dst_ref=xrecv.at[h], send_sem=xs_sem.at[h], recv_sem=xr_sem.at[h],
            device_id=partner, device_id_type=MESH,
        )

    def scatter_first(h):
        for d in range(8):
            for e in range(2):
                xsend[h, d, e] = runs[h][meta[2, d * 4 + (1 - core) * 2 + e]].astype(BF16)
        swap(h).start()

    def scatter_copy(h, d):
        return pltpu.make_async_remote_copy(
            src_ref=zsend.at[h, d - 1], dst_ref=zrecv.at[h, d - 1], send_sem=zs_sem.at[h], recv_sem=zr_sem.at[h],
            device_id=up(d), device_id_type=MESH,
        )

    def scatter_second(h):
        swap(h).wait_recv()
        for d in (4, 3, 5, 2, 6, 1, 7, 0):
            goal = (z + d) % 8
            for e in range(2):
                value = runs[h][meta[2, goal * 4 + core * 2 + e]] + xrecv[h, goal, e].astype(F32)
                if d:
                    zsend[h, d - 1, e] = value.astype(BF16)
                else:
                    own[h, e] = value
            if d:
                scatter_copy(h, d).start()

    def plain(ref, sem):
        return pltpu.make_async_copy(ref, ref, sem)

    gathered(0)
    plain(areceived.at[pl.ds(0, 15)], w_recv.at[0]).wait()
    mysum = areceived[0]
    for i in range(1, 16):
        mysum = mysum + areceived[i]
    breceived[z] = mysum
    for d in range(1, 8):
        pltpu.make_async_remote_copy(
            src_ref=breceived.at[z], dst_ref=breceived.at[z], send_sem=w_send.at[1], recv_sem=w_recv.at[1],
            device_id=up(d), device_id_type=MESH,
        ).start()

    products(0)
    scatter_first(0)

    plain(breceived.at[pl.ds(0, 7)], w_recv.at[1]).wait()
    mysum = breceived[0]
    for i in range(1, 8):
        mysum = mysum + breceived[i]
    creceived[0] = mysum
    half_sum = pltpu.make_async_remote_copy(
        src_ref=creceived.at[0], dst_ref=creceived.at[1], send_sem=w_send.at[2], recv_sem=w_recv.at[2],
        device_id=partner, device_id_type=MESH,
    )
    half_sum.start()
    scatter_second(0)

    gathered(1)
    products(1)
    scatter_first(1)

    half_sum.wait_recv()
    mine_rows = pl.ds(pl.multiple_of(col * 8, 8), 8)
    weight_grad[mine_rows, :] = creceived[0] + creceived[1]
    for a, b in plane:
        pltpu.make_async_remote_copy(
            src_ref=weight_grad.at[mine_rows], dst_ref=weight_grad.at[mine_rows],
            send_sem=w_send.at[3], recv_sem=w_recv.at[3], device_id=at(x + a, y + b), device_id_type=MESH,
        ).start()
    scatter_second(1)

    halves = []
    for h in range(2):
        plain(zrecv.at[h], zr_sem.at[h]).wait()
        pair = []
        for e in range(2):
            value = own[h, e]
            for d in range(7):
                value = value + zrecv[h, d, e].astype(F32)
            pair.append(value)
        halves.append(pair)
    for e in range(2):
        whole = jnp.concatenate([halves[0][e], halves[1][e]], axis=0)
        input_grad[e * TILE : (e + 1) * TILE, :] = whole.T.astype(BF16)

    plain(weight_grad.at[pl.ds(0, 120)], w_recv.at[3]).wait()
    plain(term.at[pl.ds(0, 120)], w_send.at[0]).wait()
    plain(breceived.at[pl.ds(0, 7)], w_send.at[1]).wait()
    half_sum.wait_send()
    plain(term.at[pl.ds(0, 120)], w_send.at[3]).wait()
    for h in range(2):
        part = aggs[h].at[pl.ds(0, 30)]
        plain(part, gather_send.at[h]).wait()
        swap(h).wait_send()
        plain(zsend.at[h], zs_sem.at[h]).wait()


def local(out_grad, relu_mask, saved_agg, weight, tile_values, tile_coords, tile_count):
    nodes = out_grad.shape[0]
    vmem, dma = pltpu.VMEM, pltpu.SemaphoreType.DMA
    return pl.pallas_call(
        kernel,
        out_shape=(
            jax.ShapeDtypeStruct((nodes, TILE), BF16),
            jax.ShapeDtypeStruct((TILE, TILE), F32),
        ),
        in_specs=[pl.BlockSpec(memory_space=pl.ANY)] * 7,
        out_specs=(pl.BlockSpec(memory_space=pltpu.VMEM), pl.BlockSpec(memory_space=pltpu.VMEM)),
        scratch_shapes=[
            vmem((nodes, TILE), BF16),
            vmem((nodes, TILE), BF16),
            vmem((nodes, TILE), BF16),
            vmem((TILE, TILE), BF16),
            vmem((SLOTS, TILE, TILE), BF16),
            vmem((2, SLOTS), jnp.int32),
            vmem((1, 1), jnp.int32),
            vmem((8, LANES), jnp.int32),
            pltpu.SMEM((8, LANES), jnp.int32),
            vmem((COLS + 1, HALF, TILE), BF16),
            vmem((COLS + 1, HALF, TILE), BF16),
            vmem((PAIRS + 1, HALF, TILE), F32),
            vmem((PAIRS + 1, HALF, TILE), F32),
            vmem((2, 8, 2, HALF, TILE), BF16),
            vmem((2, 8, 2, HALF, TILE), BF16),
            vmem((2, 7, 2, HALF, TILE), BF16),
            vmem((2, 7, 2, HALF, TILE), BF16),
            vmem((2, 2, HALF, TILE), F32),
            vmem((TILE, TILE), F32),
            vmem((16, 8, TILE), F32),
            vmem((8, 8, TILE), F32),
            vmem((2, 8, TILE), F32),
            dma((7,)),
            dma((CHUNKS,)),
            dma((12,)),
            dma((2,)),
            dma((2,)),
            dma((2,)),
            dma((2,)),
            dma((2,)),
            dma((2,)),
            dma((4,)),
            dma((4,)),
        ],
        compiler_params=pltpu.CompilerParams(
            collective_id=0, has_side_effects=True, vmem_limit_bytes=48 * 1024 * 1024
        ),
    )(out_grad, relu_mask, saved_agg, weight, tile_values, tile_coords[0, 0].T, tile_count)


def solution(mesh):
    in_specs = (
        P(("row", "col"), None),
        P(("row", "col"), None),
        P(("row", "col"), None),
        P(),
        P("row", "col", None, None, None),
        P("row", "col", None, None),
        P("row", "col"),
    )
    out_specs = (P(("col", "row"), None), P())
    return jax.shard_map(local, mesh=mesh, in_specs=in_specs, out_specs=out_specs, check_vma=False)
```

```python
import functools

import jax
import jax.numpy as jnp
from jax import lax
from jax.experimental import pallas as pl
from jax.experimental.pallas import tpu as pltpu
from jax.sharding import PartitionSpec as P

MESH = pl.DeviceIdType.MESH
F32 = jnp.float32
BF16 = jnp.bfloat16

TILE = 128
SLOTS = 320
COLS = 32
HALF = 64
PAIRS = SLOTS // 2 + COLS // 2
LANES = 384
UNROLL = 44
CHUNKS = 4


def order_slots(coords, count):
    def total(condition, value, axis):
        return jnp.sum(jnp.where(condition, value, 0), axis=axis, keepdims=True)

    def iota(shape, axis):
        return lax.broadcasted_iota(jnp.int32, shape, axis)

    square = (SLOTS, SLOTS)
    down, across = iota(square, 0), iota(square, 1)
    live = iota((1, SLOTS), 1) < jnp.broadcast_to(count, (1, SLOTS))
    row = coords[0:1, :]
    key = jnp.where(live, coords[1:2, :], COLS)
    key_all = jnp.broadcast_to(key, square)
    key_down = total(down == across, key_all, 1)
    row_down = total(down == across, jnp.broadcast_to(row, square), 1)
    rank = total((key_down == key_all) & (across < down), 1, 1)

    member = key_down == iota((SLOTS, 128), 1)
    count_lane = total(member, 1, 0)
    count_down = total(jnp.broadcast_to(key, (COLS, SLOTS)) == iota((COLS, SLOTS), 0), 1, 1)
    padded_lane = (count_lane + 1) // 2 * 2
    padded_down = (count_down + 1) // 2 * 2
    low, high = iota((COLS, 128), 0), iota((COLS, 128), 1)
    start_lane = total(low < high, padded_down, 0)
    start_down = total(high < low, padded_lane, 1)

    place = jnp.where(key_down < COLS, total(member, start_lane, 1) + rank, -1)
    payload = iota((SLOTS, 1), 0) * 64 + row_down - COLS
    packed = COLS + total(place == iota((SLOTS, LANES), 1), payload, 0)

    pair = 2 * iota((COLS, LANES), 1)
    keep = 1 - total((start_down == pair) & (count_down > 0), 1, 0)
    last = jnp.where(count_lane > 0, (start_lane + padded_lane) // 2 - 1, PAIRS)
    return packed, keep, last


def kernel(
    out_grad, relu_mask, saved_agg, weight, tile_values, coords, count, input_grad, weight_grad,
    og, rm, sa, wt, tiles, xy, ct, meta_v, meta,
    agg0, agg1, run0, run1, xsend, xrecv, zsend, zrecv, own, term, w1, w1s, w2, w3, w4,
    load_sem, tile_sem, first_recv, second_recv, gather_send,
    xs_sem, xr_sem, zs_sem, zr_sem, w_send, w_recv, near_sem,
):
    row, col = lax.axis_index("row"), lax.axis_index("col")
    z, core, x, y = row // 2, row % 2, col // 4, col % 4

    def at(xx, yy):
        return (row, xx % 4 * 4 + yy % 4)

    turn = 1 - 2 * core

    def up(d):
        return ((z + d + 8) % 8 * 2 + core, col)

    partner = (z * 2 + 1 - core, col)

    barrier = pltpu.get_barrier_semaphore()
    peers = [at(x + d, y) for d in (1, 2, 3)] + [at(x, y + d) for d in (1, 2, 3)] + [up(d) for d in (1, 2, 6, 7)] + [partner]
    for peer in peers:
        pl.semaphore_signal(barrier, inc=1, device_id=peer, device_id_type=MESH)

    loads = [
        pltpu.make_async_copy(src, dst, load_sem.at[i])
        for i, (src, dst) in enumerate(
            ((out_grad, og), (relu_mask, rm), (weight, wt), (saved_agg, sa), (coords, xy), (count, ct))
        )
    ]
    for load in loads:
        load.start()
    step = SLOTS // CHUNKS
    tile_loads = [
        pltpu.make_async_copy(
            tile_values.at[0, 0, pl.ds(i * step, step)], tiles.at[pl.ds(i * step, step)], tile_sem.at[i]
        )
        for i in range(CHUNKS)
    ]
    for load in tile_loads:
        load.start()

    aggs, runs = (agg0, agg1), (run0, run1)
    for agg in aggs:
        agg[COLS] = jnp.zeros((HALF, TILE), BF16)
    for run in runs:
        run[PAIRS] = jnp.zeros((HALF, TILE), F32)

    for load in loads[:3]:
        load.wait()
    pre = (og[...].astype(F32) * rm[...].astype(F32)).astype(BF16)
    mine = lax.dot_general(wt[...], pre, (((1,), (1,)), ((), ())), preferred_element_type=F32).astype(BF16)
    for h in range(2):
        for e in range(2):
            aggs[h][2 * col + e] = mine[h * HALF : (h + 1) * HALF, e * TILE : (e + 1) * TILE]

    pl.semaphore_wait(barrier, len(peers))
    for d in (2, 6):
        pl.semaphore_signal(near_sem, inc=1, device_id=up(d), device_id_type=MESH)

    def toward(e, phase, d):
        return at(x + d, y) if (e + phase) % 2 == 0 else at(x, y + d)

    def piece(e, d):
        a, b = ((x - d) % 4, y) if e == 0 else (x, (y - d) % 4)
        return 2 * (a * 4 + b) + e

    def gather_copy(h, r, recv, target):
        block = aggs[h].at[r]
        return pltpu.make_async_remote_copy(
            src_ref=block, dst_ref=block, send_sem=gather_send.at[h], recv_sem=recv, device_id=target, device_id_type=MESH
        )

    def second(h, e, r):
        for d in (2, 1, 3):
            gather_copy(h, r, second_recv.at[h], toward(e, 1, d)).start()

    for h in range(2):
        for e in range(2):
            for d in (2, 1, 3):
                gather_copy(h, 2 * col + e, first_recv.at[h * 6 + e * 3 + d - 1], toward(e, 0, d)).start()
        for e in range(2):
            second(h, e, 2 * col + e)

    loads[3].wait()
    term[...] = lax.dot_general(sa[...], pre, (((0,), (0,)), ((), ())), preferred_element_type=F32)

    def rows(start, size):
        return pl.ds(pl.multiple_of(start, 8), size)

    def share(i, src, dst, target):
        return pltpu.make_async_remote_copy(
            src_ref=src, dst_ref=dst, send_sem=w_send.at[i], recv_sem=w_recv.at[i], device_id=target, device_id_type=MESH
        )

    def plain(ref, sem):
        return pltpu.make_async_copy(ref, ref, sem)

    def added(ref, n):
        value = ref[0]
        for i in range(1, n):
            value = value + ref[i]
        return value

    w1[x] = term[rows(x * 32, 32), :]
    for d in (2, 1, 3):
        share(0, term.at[rows((x + d) % 4 * 32, 32)], w1.at[x], at(x + d, y)).start()

    loads[4].wait()
    loads[5].wait()
    packed, keep, last = order_slots(xy[...], ct[...])
    meta_v[...] = jnp.full((8, LANES), PAIRS, jnp.int32)
    meta_v[0:1, :] = packed
    meta_v[1:2, :] = keep
    meta_v[2:3, 0:128] = last
    to_scalar = pltpu.make_async_copy(meta_v, meta, load_sem.at[6])
    to_scalar.start()

    for h in range(2):
        for d in (1, 3, 2):
            for e in range(2):
                r = piece(e, d)
                gather_copy(h, r, first_recv.at[h * 6 + e * 3 + d - 1], toward(e, 0, d)).wait_recv()
                second(h, e, r)

    plain(w1.at[pl.ds(0, 3)], w_recv.at[0]).wait()
    w1s[...] = added(w1, 4)
    w2[y] = w1s[rows(y * 8, 8), :]
    for d in (2, 1, 3):
        share(1, w1s.at[rows((y + d) % 4 * 8, 8)], w2.at[y], at(x, y + d)).start()

    to_scalar.wait()
    for load in tile_loads:
        load.wait()

    def gathered(h):
        plain(aggs[h].at[pl.ds(0, 24)], second_recv.at[h]).wait()

    def products(h):
        agg, run = aggs[h], runs[h]

        def body(t, total):
            for u in range(UNROLL):
                q = t * UNROLL + u
                a, b = meta[0, 2 * q], meta[0, 2 * q + 1]
                left = jnp.concatenate([agg[a & 63], agg[b & 63]], axis=1)
                right = jnp.concatenate([tiles[a >> 6], tiles[b >> 6]], axis=0)
                total = total * meta[1, q].astype(F32) + jnp.dot(left, right, preferred_element_type=F32)
                run[q] = total
            return total

        lax.fori_loop(0, PAIRS // UNROLL, body, jnp.zeros((HALF, TILE), F32))

    def swap(h, far):
        part = pl.ds(5, 3) if far else pl.ds(0, 5)
        return pltpu.make_async_remote_copy(
            src_ref=xsend.at[h, part], dst_ref=xrecv.at[h, part], send_sem=xs_sem.at[h, int(far)],
            recv_sem=xr_sem.at[h, int(far)], device_id=partner, device_id_type=MESH,
        )

    def column(h, owner, k, e):
        return runs[h][meta[2, owner * 4 + k * 2 + e]]

    def scatter_swap(h):
        for far in (True, False):
            for slot in (6, 5, 7) if far else (0, 1, 3, 4, 2):
                for e in range(2):
                    xsend[h, slot, e] = column(h, (z + slot + 6) % 8, 1 - core, e).astype(BF16)
            swap(h, far).start()

    roles = (4, 3, -3, 1, -1, 2, -2)

    def scatter_copy(h, r):
        i, step = roles.index(r), {4: -2, 3: -1, -3: 1, 1: -1, -1: 1, 2: -2, -2: 2}[r]
        return pltpu.make_async_remote_copy(
            src_ref=zsend.at[h, i], dst_ref=zrecv.at[h, i], send_sem=zs_sem.at[h, i], recv_sem=zr_sem.at[h, i],
            device_id=up(turn * step), device_id_type=MESH,
        )

    def pair_sum(h, r, e):
        slot = (2 - turn * r + 8) % 8
        return column(h, (z - turn * r + 8) % 8, core, e) + xrecv[h, slot, e].astype(F32)

    def scatter_near(h):
        swap(h, True).wait_recv()
        for r in roles[:5]:
            if r == 1:
                swap(h, False).wait_recv()
            for e in range(2):
                zsend[h, roles.index(r), e] = pair_sum(h, r, e).astype(BF16)
            scatter_copy(h, r).start()
        for i, r in enumerate((2, -2, 0)):
            for e in range(2):
                own[h, i, e] = pair_sum(h, r, e)

    def scatter_far(h):
        for r, sources in ((2, (4, 3)), (-2, (-3,))):
            for q in sources:
                scatter_copy(h, q).wait_recv()
            for e in range(2):
                value = own[h, 0 if r == 2 else 1, e]
                for q in sources:
                    value = value + zrecv[h, roles.index(q), e].astype(F32)
                zsend[h, roles.index(r), e] = value.astype(BF16)
            scatter_copy(h, r).start()

    def scattered(h):
        result = []
        for r in roles[3:]:
            scatter_copy(h, r).wait_recv()
        for e in range(2):
            value = own[h, 2, e]
            for i in range(3, 7):
                value = value + zrecv[h, i, e].astype(F32)
            result.append(value)
        return result

    gathered(0)
    plain(w2.at[pl.ds(0, 3)], w_recv.at[1]).wait()
    w3[core] = added(w2, 4)
    share(2, w3.at[core], w3.at[core], partner).start()

    products(0)
    scatter_swap(0)

    share(2, w3.at[core], w3.at[1 - core], partner).wait_recv()
    w4[z] = w3[0] + w3[1]
    pl.semaphore_wait(near_sem, 2)
    for d in (4, 3, 5, 2, 6, 1, 7):
        share(3, w4.at[z], w4.at[z], up(d)).start()
    scatter_near(0)

    gathered(1)
    products(1)
    scatter_swap(1)
    scatter_far(0)
    scatter_near(1)

    plain(w4.at[pl.ds(0, 7)], w_recv.at[3]).wait()
    mine_rows = rows(x * 32 + y * 8, 8)
    weight_grad[mine_rows, :] = added(w4, 8)
    for d in (2, 1, 3):
        share(4, weight_grad.at[mine_rows], weight_grad.at[mine_rows], at(x, y + d)).start()
    first_half = scattered(0)
    scatter_far(1)
    plain(weight_grad.at[pl.ds(0, 24)], w_recv.at[4]).wait()
    line_rows = rows(x * 32, 32)
    for d in (2, 1, 3):
        share(5, weight_grad.at[line_rows], weight_grad.at[line_rows], at(x + d, y)).start()

    second_half = scattered(1)
    for e in range(2):
        whole = jnp.concatenate([first_half[e], second_half[e]], axis=0)
        input_grad[e * TILE : (e + 1) * TILE, :] = whole.T.astype(BF16)

    plain(weight_grad.at[pl.ds(0, 96)], w_recv.at[5]).wait()
    for i, size in enumerate((96, 24, 8, 56, 24, 96)):
        plain(term.at[pl.ds(0, size)], w_send.at[i]).wait()
    for h in range(2):
        plain(aggs[h].at[pl.ds(0, 30)], gather_send.at[h]).wait()
        for far in (True, False):
            swap(h, far).wait_send()
        for r in roles:
            scatter_copy(h, r).wait_send()


def local(out_grad, relu_mask, saved_agg, weight, tile_values, tile_coords, tile_count):
    nodes = out_grad.shape[0]
    vmem, dma = pltpu.VMEM, pltpu.SemaphoreType.DMA
    return pl.pallas_call(
        kernel,
        out_shape=(
            pltpu.VMEM((nodes, TILE), BF16),
            pltpu.VMEM((TILE, TILE), F32),
        ),
        in_specs=[pl.BlockSpec(memory_space=pltpu.HBM)] * 7,
        out_specs=(pl.BlockSpec(memory_space=pltpu.VMEM), pl.BlockSpec(memory_space=pltpu.VMEM)),
        scratch_shapes=[
            vmem((nodes, TILE), BF16),
            vmem((nodes, TILE), BF16),
            vmem((nodes, TILE), BF16),
            vmem((TILE, TILE), BF16),
            vmem((SLOTS, TILE, TILE), BF16),
            vmem((2, SLOTS), jnp.int32),
            vmem((1, 1), jnp.int32),
            vmem((8, LANES), jnp.int32),
            pltpu.SMEM((8, LANES), jnp.int32),
            vmem((COLS + 1, HALF, TILE), BF16),
            vmem((COLS + 1, HALF, TILE), BF16),
            vmem((PAIRS + 1, HALF, TILE), F32),
            vmem((PAIRS + 1, HALF, TILE), F32),
            vmem((2, 8, 2, HALF, TILE), BF16),
            vmem((2, 8, 2, HALF, TILE), BF16),
            vmem((2, 7, 2, HALF, TILE), BF16),
            vmem((2, 7, 2, HALF, TILE), BF16),
            vmem((2, 3, 2, HALF, TILE), F32),
            vmem((TILE, TILE), F32),
            vmem((4, 32, TILE), F32),
            vmem((32, TILE), F32),
            vmem((4, 8, TILE), F32),
            vmem((2, 8, TILE), F32),
            vmem((8, 8, TILE), F32),
            dma((7,)),
            dma((CHUNKS,)),
            dma((12,)),
            dma((2,)),
            dma((2,)),
            dma((2, 2)),
            dma((2, 2)),
            dma((2, 7)),
            dma((2, 7)),
            dma((6,)),
            dma((6,)),
            pltpu.SemaphoreType.REGULAR,
        ],
        compiler_params=pltpu.CompilerParams(
            collective_id=0, has_side_effects=True, vmem_limit_bytes=48 * 1024 * 1024
        ),
    )(*[
        pltpu.with_memory_space_constraint(array, pltpu.HBM)
        for array in (out_grad, relu_mask, saved_agg, weight, tile_values, tile_coords[0, 0].T)
    ], tile_count)


def solution(mesh):
    in_specs = (
        P(("row", "col"), None),
        P(("row", "col"), None),
        P(("row", "col"), None),
        P(),
        P("row", "col", None, None, None),
        P("row", "col", None, None),
        P("row", "col"),
    )
    out_specs = (P(("col", "row"), None), P())
    return jax.shard_map(local, mesh=mesh, in_specs=in_specs, out_specs=out_specs, check_vma=False)
```

```python
import functools

import jax
import jax.numpy as jnp
from jax import lax
from jax.experimental import pallas as pl
from jax.experimental.pallas import tpu as pltpu
from jax.sharding import PartitionSpec as P

MESH = pl.DeviceIdType.MESH
F32 = jnp.float32
BF16 = jnp.bfloat16

TILE = 128
SLOTS = 320
COLS = 32
HALF = 64
PAIRS = SLOTS // 2 + COLS // 2
LANES = 384
UNROLL = 88
CHUNKS = 4


def order_slots(coords, count):
    def total(condition, value, axis):
        return jnp.sum(jnp.where(condition, value, 0), axis=axis, keepdims=True)

    def iota(shape, axis):
        return lax.broadcasted_iota(jnp.int32, shape, axis)

    square = (SLOTS, SLOTS)
    down, across = iota(square, 0), iota(square, 1)
    live = iota((1, SLOTS), 1) < jnp.broadcast_to(count, (1, SLOTS))
    row = coords[0:1, :]
    key = jnp.where(live, coords[1:2, :], COLS)
    key_all = jnp.broadcast_to(key, square)
    key_down = total(down == across, key_all, 1)
    row_down = total(down == across, jnp.broadcast_to(row, square), 1)
    rank = total((key_down == key_all) & (across < down), 1, 1)

    member = key_down == iota((SLOTS, 128), 1)
    count_lane = total(member, 1, 0)
    count_down = total(jnp.broadcast_to(key, (COLS, SLOTS)) == iota((COLS, SLOTS), 0), 1, 1)
    padded_lane = (count_lane + 1) // 2 * 2
    padded_down = (count_down + 1) // 2 * 2
    low, high = iota((COLS, 128), 0), iota((COLS, 128), 1)
    start_lane = total(low < high, padded_down, 0)
    start_down = total(high < low, padded_lane, 1)

    place = jnp.where(key_down < COLS, total(member, start_lane, 1) + rank, -1)
    payload = iota((SLOTS, 1), 0) * 64 + row_down - COLS
    packed = COLS + total(place == iota((SLOTS, LANES), 1), payload, 0)

    pair = 2 * iota((COLS, LANES), 1)
    keep = 1 - total((start_down == pair) & (count_down > 0), 1, 0)
    last = jnp.where(count_lane > 0, (start_lane + padded_lane) // 2 - 1, PAIRS)
    return packed, keep, last


def kernel(
    out_grad, relu_mask, saved_agg, weight, tile_values, coords, count, input_grad, weight_grad,
    og, rm, sa, wt, tiles, xy, ct, meta_v, meta,
    agg0, agg1, run0, run1, xsend, xrecv, zsend, zrecv, own, term, w1, w1s, w2, w3, w4,
    load_sem, tile_sem, first_recv, second_recv, gather_send,
    xs_sem, xr_sem, zs_sem, zr_sem, w_send, w_recv, near_sem,
):
    row, col = lax.axis_index("row"), lax.axis_index("col")
    z, core, x, y = row // 2, row % 2, col // 4, col % 4

    def at(xx, yy):
        return (row, xx % 4 * 4 + yy % 4)

    turn = 1 - 2 * core

    def up(d):
        return ((z + d + 8) % 8 * 2 + core, col)

    partner = (z * 2 + 1 - core, col)

    barrier = pltpu.get_barrier_semaphore()
    peers = [at(x + d, y) for d in (1, 2, 3)] + [at(x, y + d) for d in (1, 2, 3)] + [up(d) for d in (1, 2, 6, 7)] + [partner]
    for peer in peers:
        pl.semaphore_signal(barrier, inc=1, device_id=peer, device_id_type=MESH)

    loads = [
        pltpu.make_async_copy(src, dst, load_sem.at[i])
        for i, (src, dst) in enumerate(
            ((out_grad, og), (relu_mask, rm), (weight, wt), (saved_agg, sa), (coords, xy), (count, ct))
        )
    ]
    for load in loads:
        load.start()
    step = SLOTS // CHUNKS
    tile_loads = [
        pltpu.make_async_copy(
            tile_values.at[0, 0, pl.ds(i * step, step)], tiles.at[pl.ds(i * step, step)], tile_sem.at[i]
        )
        for i in range(CHUNKS)
    ]
    for load in tile_loads:
        load.start()

    aggs, runs = (agg0, agg1), (run0, run1)
    for agg in aggs:
        agg[COLS] = jnp.zeros((HALF, TILE), BF16)
    for run in runs:
        run[PAIRS] = jnp.zeros((HALF, TILE), F32)

    for load in loads[:3]:
        load.wait()
    pre = (og[...].astype(F32) * rm[...].astype(F32)).astype(BF16)
    mine = lax.dot_general(wt[...], pre, (((1,), (1,)), ((), ())), preferred_element_type=F32).astype(BF16)
    for h in range(2):
        for e in range(2):
            aggs[h][2 * col + e] = mine[h * HALF : (h + 1) * HALF, e * TILE : (e + 1) * TILE]

    pl.semaphore_wait(barrier, len(peers))
    for d in (2, 6):
        pl.semaphore_signal(near_sem, inc=1, device_id=up(d), device_id_type=MESH)

    def toward(e, phase, d):
        return at(x + d, y) if (e + phase) % 2 == 0 else at(x, y + d)

    def piece(e, d):
        a, b = ((x - d) % 4, y) if e == 0 else (x, (y - d) % 4)
        return 2 * (a * 4 + b) + e

    def gather_copy(h, r, recv, target):
        block = aggs[h].at[r]
        return pltpu.make_async_remote_copy(
            src_ref=block, dst_ref=block, send_sem=gather_send.at[h], recv_sem=recv, device_id=target, device_id_type=MESH
        )

    def second(h, e, r):
        for d in (2, 1, 3):
            gather_copy(h, r, second_recv.at[h], toward(e, 1, d)).start()

    for h in range(2):
        for e in range(2):
            for d in (2, 1, 3):
                gather_copy(h, 2 * col + e, first_recv.at[h * 6 + e * 3 + d - 1], toward(e, 0, d)).start()
        for e in range(2):
            second(h, e, 2 * col + e)

    loads[3].wait()
    term[...] = lax.dot_general(sa[...], pre, (((0,), (0,)), ((), ())), preferred_element_type=F32)

    def rows(start, size):
        return pl.ds(pl.multiple_of(start, 8), size)

    def share(i, src, dst, target):
        return pltpu.make_async_remote_copy(
            src_ref=src, dst_ref=dst, send_sem=w_send.at[i], recv_sem=w_recv.at[i], device_id=target, device_id_type=MESH
        )

    def plain(ref, sem):
        return pltpu.make_async_copy(ref, ref, sem)

    def added(ref, n):
        value = ref[0]
        for i in range(1, n):
            value = value + ref[i]
        return value

    half_rows = rows(core * 64, 64)
    share(0, term.at[rows((1 - core) * 64, 64)], w1, partner).start()

    loads[4].wait()
    loads[5].wait()
    packed, keep, last = order_slots(xy[...], ct[...])
    meta_v[...] = jnp.full((8, LANES), PAIRS, jnp.int32)
    meta_v[0:1, :] = packed
    meta_v[1:2, :] = keep
    meta_v[2:3, 0:128] = last
    to_scalar = pltpu.make_async_copy(meta_v, meta, load_sem.at[6])
    to_scalar.start()

    for h in range(2):
        for d in (1, 3, 2):
            for e in range(2):
                r = piece(e, d)
                gather_copy(h, r, first_recv.at[h * 6 + e * 3 + d - 1], toward(e, 0, d)).wait_recv()
                second(h, e, r)

    share(0, w1, w1, partner).wait_recv()
    w1s[...] = term[half_rows, :] + w1[...]
    w2[z] = w1s[rows(z * 8, 8), :]
    pl.semaphore_wait(near_sem, 2)
    for d in (4, 3, 5, 2, 6, 1, 7):
        share(1, w1s.at[rows((z + d) % 8 * 8, 8)], w2.at[z], up(d)).start()

    to_scalar.wait()
    for load in tile_loads:
        load.wait()

    def gathered(h):
        plain(aggs[h].at[pl.ds(0, 24)], second_recv.at[h]).wait()

    def products(h):
        agg, run = aggs[h], runs[h]

        def body(t, total):
            for u in range(UNROLL):
                q = t * UNROLL + u
                a, b = meta[0, 2 * q], meta[0, 2 * q + 1]
                left = jnp.concatenate([agg[a & 63], agg[b & 63]], axis=1)
                right = jnp.concatenate([tiles[a >> 6], tiles[b >> 6]], axis=0)
                total = total * meta[1, q].astype(F32) + jnp.dot(left, right, preferred_element_type=F32)
                run[q] = total
            return total

        lax.fori_loop(0, PAIRS // UNROLL, body, jnp.zeros((HALF, TILE), F32))

    def swap(h, far):
        part = pl.ds(5, 3) if far else pl.ds(0, 5)
        return pltpu.make_async_remote_copy(
            src_ref=xsend.at[h, part], dst_ref=xrecv.at[h, part], send_sem=xs_sem.at[h, int(far)],
            recv_sem=xr_sem.at[h, int(far)], device_id=partner, device_id_type=MESH,
        )

    def column(h, owner, k, e):
        return runs[h][meta[2, owner * 4 + k * 2 + e]]

    def scatter_swap(h):
        for far in (True, False):
            for slot in (6, 5, 7) if far else (0, 1, 3, 4, 2):
                for e in range(2):
                    xsend[h, slot, e] = column(h, (z + slot + 6) % 8, 1 - core, e).astype(BF16)
            swap(h, far).start()

    roles = (4, 3, -3, 1, -1, 2, -2)

    def scatter_copy(h, r):
        i, step = roles.index(r), {4: -2, 3: -1, -3: 1, 1: -1, -1: 1, 2: -2, -2: 2}[r]
        return pltpu.make_async_remote_copy(
            src_ref=zsend.at[h, i], dst_ref=zrecv.at[h, i], send_sem=zs_sem.at[h, i], recv_sem=zr_sem.at[h, i],
            device_id=up(turn * step), device_id_type=MESH,
        )

    def pair_sum(h, r, e):
        slot = (2 - turn * r + 8) % 8
        return column(h, (z - turn * r + 8) % 8, core, e) + xrecv[h, slot, e].astype(F32)

    def scatter_near(h):
        swap(h, True).wait_recv()
        for r in roles[:5]:
            if r == 1:
                swap(h, False).wait_recv()
            for e in range(2):
                zsend[h, roles.index(r), e] = pair_sum(h, r, e).astype(BF16)
            scatter_copy(h, r).start()
        for i, r in enumerate((2, -2, 0)):
            for e in range(2):
                own[h, i, e] = pair_sum(h, r, e)

    def scatter_far(h):
        for r, sources in ((2, (4, 3)), (-2, (-3,))):
            for q in sources:
                scatter_copy(h, q).wait_recv()
            for e in range(2):
                value = own[h, 0 if r == 2 else 1, e]
                for q in sources:
                    value = value + zrecv[h, roles.index(q), e].astype(F32)
                zsend[h, roles.index(r), e] = value.astype(BF16)
            scatter_copy(h, r).start()

    def scattered(h):
        result = []
        for r in roles[3:]:
            scatter_copy(h, r).wait_recv()
        for e in range(2):
            value = own[h, 2, e]
            for i in range(3, 7):
                value = value + zrecv[h, i, e].astype(F32)
            result.append(value)
        return result

    gathered(0)
    products(0)
    scatter_swap(0)
    plain(w2.at[pl.ds(0, 7)], w_recv.at[1]).wait()
    w3[x] = added(w2, 8)
    for d in (2, 1, 3):
        share(2, w3.at[x], w3.at[x], at(x + d, y)).start()
    scatter_near(0)
    gathered(1)
    products(1)
    scatter_swap(1)
    plain(w3.at[pl.ds(0, 3)], w_recv.at[2]).wait()
    w4[y] = added(w3, 4)
    for d in (2, 1, 3):
        share(3, w4.at[y], w4.at[y], at(x, y + d)).start()
    scatter_near(1)
    scatter_far(0)
    plain(w4.at[pl.ds(0, 3)], w_recv.at[3]).wait()
    mine_rows = rows(core * 64 + z * 8, 8)
    weight_grad[mine_rows, :] = added(w4, 4)
    for d in (4, 3, 5, 2, 6, 1, 7):
        share(4, weight_grad.at[mine_rows], weight_grad.at[mine_rows], up(d)).start()
    scatter_far(1)

    first_half = scattered(0)
    plain(weight_grad.at[pl.ds(0, 56)], w_recv.at[4]).wait()
    share(5, weight_grad.at[half_rows], weight_grad.at[half_rows], partner).start()
    second_half = scattered(1)
    for e in range(2):
        whole = jnp.concatenate([first_half[e], second_half[e]], axis=0)
        input_grad[e * TILE : (e + 1) * TILE, :] = whole.T.astype(BF16)

    plain(weight_grad.at[pl.ds(0, 64)], w_recv.at[5]).wait()
    for i, size in enumerate((64, 56, 24, 24, 56, 64)):
        plain(term.at[pl.ds(0, size)], w_send.at[i]).wait()
    for h in range(2):
        plain(aggs[h].at[pl.ds(0, 30)], gather_send.at[h]).wait()
        for far in (True, False):
            swap(h, far).wait_send()
        for r in roles:
            scatter_copy(h, r).wait_send()


def write_out(input_grad, weight_grad, input_out, weight_out, sems):
    copies = [
        pltpu.make_async_copy(input_grad, input_out, sems.at[0]),
        pltpu.make_async_copy(weight_grad, weight_out, sems.at[1]),
    ]
    for copy in copies:
        copy.start()
    for copy in copies:
        copy.wait()


def local(out_grad, relu_mask, saved_agg, weight, tile_values, tile_coords, tile_count):
    nodes = out_grad.shape[0]
    vmem, dma = pltpu.VMEM, pltpu.SemaphoreType.DMA
    results = pl.pallas_call(
        kernel,
        out_shape=(
            pltpu.VMEM((nodes, TILE), BF16),
            pltpu.VMEM((TILE, TILE), F32),
        ),
        in_specs=[pl.BlockSpec(memory_space=pltpu.HBM)] * 7,
        out_specs=(pl.BlockSpec(memory_space=pltpu.VMEM), pl.BlockSpec(memory_space=pltpu.VMEM)),
        scratch_shapes=[
            vmem((nodes, TILE), BF16),
            vmem((nodes, TILE), BF16),
            vmem((nodes, TILE), BF16),
            vmem((TILE, TILE), BF16),
            vmem((SLOTS, TILE, TILE), BF16),
            vmem((2, SLOTS), jnp.int32),
            vmem((1, 1), jnp.int32),
            vmem((8, LANES), jnp.int32),
            pltpu.SMEM((8, LANES), jnp.int32),
            vmem((COLS + 1, HALF, TILE), BF16),
            vmem((COLS + 1, HALF, TILE), BF16),
            vmem((PAIRS + 1, HALF, TILE), F32),
            vmem((PAIRS + 1, HALF, TILE), F32),
            vmem((2, 8, 2, HALF, TILE), BF16),
            vmem((2, 8, 2, HALF, TILE), BF16),
            vmem((2, 7, 2, HALF, TILE), BF16),
            vmem((2, 7, 2, HALF, TILE), BF16),
            vmem((2, 3, 2, HALF, TILE), F32),
            vmem((TILE, TILE), F32),
            vmem((64, TILE), F32),
            vmem((64, TILE), F32),
            vmem((8, 8, TILE), F32),
            vmem((4, 8, TILE), F32),
            vmem((4, 8, TILE), F32),
            dma((7,)),
            dma((CHUNKS,)),
            dma((12,)),
            dma((2,)),
            dma((2,)),
            dma((2, 2)),
            dma((2, 2)),
            dma((2, 7)),
            dma((2, 7)),
            dma((6,)),
            dma((6,)),
            pltpu.SemaphoreType.REGULAR,
        ],
        compiler_params=pltpu.CompilerParams(
            collective_id=0, has_side_effects=True, vmem_limit_bytes=48 * 1024 * 1024
        ),
    )(*[
        pltpu.with_memory_space_constraint(array, pltpu.HBM)
        for array in (out_grad, relu_mask, saved_agg, weight, tile_values, tile_coords[0, 0].T)
    ], tile_count)
    return pl.pallas_call(
        write_out,
        out_shape=(pltpu.HBM((nodes, TILE), BF16), pltpu.HBM((TILE, TILE), F32)),
        in_specs=[pl.BlockSpec(memory_space=pltpu.VMEM)] * 2,
        out_specs=[pl.BlockSpec(memory_space=pltpu.HBM)] * 2,
        scratch_shapes=[dma((2,))],
    )(*[pltpu.with_memory_space_constraint(result, pltpu.VMEM) for result in results])


def solution(mesh):
    in_specs = (
        P(("row", "col"), None),
        P(("row", "col"), None),
        P(("row", "col"), None),
        P(),
        P("row", "col", None, None, None),
        P("row", "col", None, None),
        P("row", "col"),
    )
    out_specs = (P(("col", "row"), None), P())
    return jax.shard_map(local, mesh=mesh, in_specs=in_specs, out_specs=out_specs, check_vma=False)
```

```python
import functools

import jax
import jax.numpy as jnp
from jax import lax
from jax.experimental import pallas as pl
from jax.experimental.pallas import tpu as pltpu
from jax.sharding import PartitionSpec as P

MESH = pl.DeviceIdType.MESH
F32 = jnp.float32
BF16 = jnp.bfloat16

TILE = 128
SLOTS = 320
COLS = 32
HALF = 64
PAIRS = SLOTS // 2 + COLS // 2
LANES = 384
UNROLL = 88
CHUNKS = 4


def order_slots(coords, count):
    def total(condition, value, axis):
        return jnp.sum(jnp.where(condition, value, 0), axis=axis, keepdims=True)

    def iota(shape, axis):
        return lax.broadcasted_iota(jnp.int32, shape, axis)

    square = (SLOTS, SLOTS)
    down, across = iota(square, 0), iota(square, 1)
    live = iota((1, SLOTS), 1) < jnp.broadcast_to(count, (1, SLOTS))
    row = coords[0:1, :]
    key = jnp.where(live, coords[1:2, :], COLS)
    key_all = jnp.broadcast_to(key, square)
    key_down = total(down == across, key_all, 1)
    row_down = total(down == across, jnp.broadcast_to(row, square), 1)
    rank = total((key_down == key_all) & (across < down), 1, 1)

    member = key_down == iota((SLOTS, 128), 1)
    count_lane = total(member, 1, 0)
    count_down = total(jnp.broadcast_to(key, (COLS, SLOTS)) == iota((COLS, SLOTS), 0), 1, 1)
    padded_lane = (count_lane + 1) // 2 * 2
    padded_down = (count_down + 1) // 2 * 2
    low, high = iota((COLS, 128), 0), iota((COLS, 128), 1)
    start_lane = total(low < high, padded_down, 0)
    start_down = total(high < low, padded_lane, 1)

    place = jnp.where(key_down < COLS, total(member, start_lane, 1) + rank, -1)
    payload = iota((SLOTS, 1), 0) * 64 + row_down - COLS
    packed = COLS + total(place == iota((SLOTS, LANES), 1), payload, 0)

    pair = 2 * iota((COLS, LANES), 1)
    keep = 1 - total((start_down == pair) & (count_down > 0), 1, 0)
    last = jnp.where(count_lane > 0, (start_lane + padded_lane) // 2 - 1, PAIRS)
    return packed, keep, last


def kernel(
    out_grad, relu_mask, saved_agg, weight, tile_values, coords, count, input_grad, weight_grad,
    og, rm, sa, wt, tiles, xy, ct, meta_v, meta,
    agg0, agg1, run0, run1, xsend, xrecv, zsend, zrecv, own, term, w1, w1s, w2, w3,
    load_sem, tile_sem, first_recv, second_recv, gather_send,
    xs_sem, xr_sem, zs_sem, zr_sem, w_send, w_recv, near_sem,
):
    row, col = lax.axis_index("row"), lax.axis_index("col")
    z, core, x, y = row // 2, row % 2, col // 4, col % 4

    def at(xx, yy):
        return (row, xx % 4 * 4 + yy % 4)

    turn = 1 - 2 * core

    def up(d):
        return ((z + d + 8) % 8 * 2 + core, col)

    partner = (z * 2 + 1 - core, col)

    barrier = pltpu.get_barrier_semaphore()
    peers = [at(x + d, y) for d in (1, 2, 3)] + [at(x, y + d) for d in (1, 2, 3)] + [up(d) for d in (1, 2, 6, 7)] + [partner]
    for peer in peers:
        pl.semaphore_signal(barrier, inc=1, device_id=peer, device_id_type=MESH)

    loads = [
        pltpu.make_async_copy(src, dst, load_sem.at[i])
        for i, (src, dst) in enumerate(
            ((out_grad, og), (relu_mask, rm), (weight, wt), (saved_agg, sa), (coords, xy), (count, ct))
        )
    ]
    for load in loads:
        load.start()
    step = SLOTS // CHUNKS
    tile_loads = [
        pltpu.make_async_copy(
            tile_values.at[0, 0, pl.ds(i * step, step)], tiles.at[pl.ds(i * step, step)], tile_sem.at[i]
        )
        for i in range(CHUNKS)
    ]
    for load in tile_loads:
        load.start()

    aggs, runs = (agg0, agg1), (run0, run1)
    for agg in aggs:
        agg[COLS] = jnp.zeros((HALF, TILE), BF16)
    for run in runs:
        run[PAIRS] = jnp.zeros((HALF, TILE), F32)

    for load in loads[:3]:
        load.wait()
    pre = (og[...].astype(F32) * rm[...].astype(F32)).astype(BF16)
    mine = lax.dot_general(wt[...], pre, (((1,), (1,)), ((), ())), preferred_element_type=F32).astype(BF16)
    for h in range(2):
        for e in range(2):
            aggs[h][2 * col + e] = mine[h * HALF : (h + 1) * HALF, e * TILE : (e + 1) * TILE]

    pl.semaphore_wait(barrier, len(peers))
    for d in (2, 6):
        pl.semaphore_signal(near_sem, inc=1, device_id=up(d), device_id_type=MESH)

    def toward(e, phase, d):
        return at(x + d, y) if (e + phase) % 2 == 0 else at(x, y + d)

    def piece(e, d):
        a, b = ((x - d) % 4, y) if e == 0 else (x, (y - d) % 4)
        return 2 * (a * 4 + b) + e

    def gather_copy(h, r, recv, target):
        block = aggs[h].at[r]
        return pltpu.make_async_remote_copy(
            src_ref=block, dst_ref=block, send_sem=gather_send.at[h], recv_sem=recv, device_id=target, device_id_type=MESH
        )

    def second(h, e, r):
        for d in (2, 1, 3):
            gather_copy(h, r, second_recv.at[h], toward(e, 1, d)).start()

    for h in range(2):
        for e in range(2):
            for d in (2, 1, 3):
                gather_copy(h, 2 * col + e, first_recv.at[h * 6 + e * 3 + d - 1], toward(e, 0, d)).start()
        for e in range(2):
            second(h, e, 2 * col + e)

    loads[3].wait()
    term[...] = lax.dot_general(sa[...], pre, (((0,), (0,)), ((), ())), preferred_element_type=F32)

    def rows(start, size):
        return pl.ds(pl.multiple_of(start, 8), size)

    def share(i, src, dst, target):
        return pltpu.make_async_remote_copy(
            src_ref=src, dst_ref=dst, send_sem=w_send.at[i], recv_sem=w_recv.at[i], device_id=target, device_id_type=MESH
        )

    def plain(ref, sem):
        return pltpu.make_async_copy(ref, ref, sem)

    def added(ref, n):
        value = ref[0]
        for i in range(1, n):
            value = value + ref[i]
        return value

    half_rows = rows(core * 64, 64)
    share(0, term.at[rows((1 - core) * 64, 64)], w1, partner).start()

    loads[4].wait()
    loads[5].wait()
    packed, keep, last = order_slots(xy[...], ct[...])
    meta_v[...] = jnp.full((8, LANES), PAIRS, jnp.int32)
    meta_v[0:1, :] = packed
    meta_v[1:2, :] = keep
    meta_v[2:3, 0:128] = last
    to_scalar = pltpu.make_async_copy(meta_v, meta, load_sem.at[6])
    to_scalar.start()

    share(0, w1, w1, partner).wait_recv()
    w1s[...] = term[half_rows, :] + w1[...]
    w2[z] = w1s[rows(z * 8, 8), :]
    pl.semaphore_wait(near_sem, 2)
    for d in (4, 3, 5, 2, 6, 1, 7):
        share(1, w1s.at[rows((z + d) % 8 * 8, 8)], w2.at[z], up(d)).start()

    for h in range(2):
        for d in (1, 3, 2):
            for e in range(2):
                r = piece(e, d)
                gather_copy(h, r, first_recv.at[h * 6 + e * 3 + d - 1], toward(e, 0, d)).wait_recv()
                second(h, e, r)

    to_scalar.wait()
    for load in tile_loads:
        load.wait()

    def gathered(h):
        plain(aggs[h].at[pl.ds(0, 24)], second_recv.at[h]).wait()

    def products(h):
        agg, run = aggs[h], runs[h]

        def body(t, total):
            for u in range(UNROLL):
                q = t * UNROLL + u
                a, b = meta[0, 2 * q], meta[0, 2 * q + 1]
                left = jnp.concatenate([agg[a & 63], agg[b & 63]], axis=1)
                right = jnp.concatenate([tiles[a >> 6], tiles[b >> 6]], axis=0)
                total = total * meta[1, q].astype(F32) + jnp.dot(left, right, preferred_element_type=F32)
                run[q] = total
            return total

        lax.fori_loop(0, PAIRS // UNROLL, body, jnp.zeros((HALF, TILE), F32))

    def swap(h, far):
        part = pl.ds(5, 3) if far else pl.ds(0, 5)
        return pltpu.make_async_remote_copy(
            src_ref=xsend.at[h, part], dst_ref=xrecv.at[h, part], send_sem=xs_sem.at[h, int(far)],
            recv_sem=xr_sem.at[h, int(far)], device_id=partner, device_id_type=MESH,
        )

    def column(h, owner, k, e):
        return runs[h][meta[2, owner * 4 + k * 2 + e]]

    def scatter_swap(h):
        for far in (True, False):
            for slot in (6, 5, 7) if far else (0, 1, 3, 4, 2):
                for e in range(2):
                    xsend[h, slot, e] = column(h, (z + slot + 6) % 8, 1 - core, e).astype(BF16)
            swap(h, far).start()

    roles = (4, 3, -3, 1, -1, 2, -2)

    def scatter_copy(h, r):
        i, step = roles.index(r), {4: -2, 3: -1, -3: 1, 1: -1, -1: 1, 2: -2, -2: 2}[r]
        return pltpu.make_async_remote_copy(
            src_ref=zsend.at[h, i], dst_ref=zrecv.at[h, i], send_sem=zs_sem.at[h, i], recv_sem=zr_sem.at[h, i],
            device_id=up(turn * step), device_id_type=MESH,
        )

    def pair_sum(h, r, e):
        slot = (2 - turn * r + 8) % 8
        return column(h, (z - turn * r + 8) % 8, core, e) + xrecv[h, slot, e].astype(F32)

    def scatter_near(h):
        swap(h, True).wait_recv()
        for r in roles[:5]:
            if r == 1:
                swap(h, False).wait_recv()
            for e in range(2):
                zsend[h, roles.index(r), e] = pair_sum(h, r, e).astype(BF16)
            scatter_copy(h, r).start()
        for i, r in enumerate((2, -2, 0)):
            for e in range(2):
                own[h, i, e] = pair_sum(h, r, e)

    def scatter_far(h):
        for r, sources in ((2, (4, 3)), (-2, (-3,))):
            for q in sources:
                scatter_copy(h, q).wait_recv()
            for e in range(2):
                value = own[h, 0 if r == 2 else 1, e]
                for q in sources:
                    value = value + zrecv[h, roles.index(q), e].astype(F32)
                zsend[h, roles.index(r), e] = value.astype(BF16)
            scatter_copy(h, r).start()

    def scattered(h):
        result = []
        for r in roles[3:]:
            scatter_copy(h, r).wait_recv()
        for e in range(2):
            value = own[h, 2, e]
            for i in range(3, 7):
                value = value + zrecv[h, i, e].astype(F32)
            result.append(value)
        return result

    gathered(0)
    plain(w2.at[pl.ds(0, 7)], w_recv.at[1]).wait()
    w3[col] = added(w2, 8)
    for a, b in ((2, 2), (1, 2), (3, 2), (2, 1), (2, 3), (0, 2), (2, 0), (1, 1), (1, 3), (3, 1), (3, 3), (0, 1), (0, 3), (1, 0), (3, 0)):
        share(2, w3.at[col], w3.at[col], at(x + a, y + b)).start()
    products(0)
    scatter_swap(0)
    scatter_near(0)
    gathered(1)
    products(1)
    scatter_swap(1)
    plain(w3.at[pl.ds(0, 15)], w_recv.at[2]).wait()
    mine_rows = rows(core * 64 + z * 8, 8)
    weight_grad[mine_rows, :] = added(w3, 16)
    for d in (4, 3, 5, 2, 6, 1, 7):
        share(4, weight_grad.at[mine_rows], weight_grad.at[mine_rows], up(d)).start()
    scatter_near(1)
    scatter_far(0)
    scatter_far(1)

    first_half = scattered(0)
    plain(weight_grad.at[pl.ds(0, 56)], w_recv.at[4]).wait()
    share(5, weight_grad.at[half_rows], weight_grad.at[half_rows], partner).start()
    second_half = scattered(1)
    for e in range(2):
        whole = jnp.concatenate([first_half[e], second_half[e]], axis=0)
        input_grad[e * TILE : (e + 1) * TILE, :] = whole.T.astype(BF16)

    plain(weight_grad.at[pl.ds(0, 64)], w_recv.at[5]).wait()
    for i, size in ((0, 64), (1, 56), (2, 120), (4, 56), (5, 64)):
        plain(term.at[pl.ds(0, size)], w_send.at[i]).wait()
    for h in range(2):
        plain(aggs[h].at[pl.ds(0, 30)], gather_send.at[h]).wait()
        for far in (True, False):
            swap(h, far).wait_send()
        for r in roles:
            scatter_copy(h, r).wait_send()


def write_out(input_grad, weight_grad, input_out, weight_out, sems):
    copies = [
        pltpu.make_async_copy(input_grad, input_out, sems.at[0]),
        pltpu.make_async_copy(weight_grad, weight_out, sems.at[1]),
    ]
    for copy in copies:
        copy.start()
    for copy in copies:
        copy.wait()


def local(out_grad, relu_mask, saved_agg, weight, tile_values, tile_coords, tile_count):
    nodes = out_grad.shape[0]
    vmem, dma = pltpu.VMEM, pltpu.SemaphoreType.DMA
    results = pl.pallas_call(
        kernel,
        out_shape=(
            pltpu.VMEM((nodes, TILE), BF16),
            pltpu.VMEM((TILE, TILE), F32),
        ),
        in_specs=[pl.BlockSpec(memory_space=pltpu.HBM)] * 7,
        out_specs=(pl.BlockSpec(memory_space=pltpu.VMEM), pl.BlockSpec(memory_space=pltpu.VMEM)),
        scratch_shapes=[
            vmem((nodes, TILE), BF16),
            vmem((nodes, TILE), BF16),
            vmem((nodes, TILE), BF16),
            vmem((TILE, TILE), BF16),
            vmem((SLOTS, TILE, TILE), BF16),
            vmem((2, SLOTS), jnp.int32),
            vmem((1, 1), jnp.int32),
            vmem((8, LANES), jnp.int32),
            pltpu.SMEM((8, LANES), jnp.int32),
            vmem((COLS + 1, HALF, TILE), BF16),
            vmem((COLS + 1, HALF, TILE), BF16),
            vmem((PAIRS + 1, HALF, TILE), F32),
            vmem((PAIRS + 1, HALF, TILE), F32),
            vmem((2, 8, 2, HALF, TILE), BF16),
            vmem((2, 8, 2, HALF, TILE), BF16),
            vmem((2, 7, 2, HALF, TILE), BF16),
            vmem((2, 7, 2, HALF, TILE), BF16),
            vmem((2, 3, 2, HALF, TILE), F32),
            vmem((TILE, TILE), F32),
            vmem((64, TILE), F32),
            vmem((64, TILE), F32),
            vmem((8, 8, TILE), F32),
            vmem((16, 8, TILE), F32),
            dma((7,)),
            dma((CHUNKS,)),
            dma((12,)),
            dma((2,)),
            dma((2,)),
            dma((2, 2)),
            dma((2, 2)),
            dma((2, 7)),
            dma((2, 7)),
            dma((6,)),
            dma((6,)),
            pltpu.SemaphoreType.REGULAR,
        ],
        compiler_params=pltpu.CompilerParams(
            collective_id=0, has_side_effects=True, vmem_limit_bytes=48 * 1024 * 1024
        ),
    )(*[
        pltpu.with_memory_space_constraint(array, pltpu.HBM)
        for array in (out_grad, relu_mask, saved_agg, weight, tile_values, tile_coords[0, 0].T)
    ], tile_count)
    return pl.pallas_call(
        write_out,
        out_shape=(pltpu.HBM((nodes, TILE), BF16), pltpu.HBM((TILE, TILE), F32)),
        in_specs=[pl.BlockSpec(memory_space=pltpu.VMEM)] * 2,
        out_specs=[pl.BlockSpec(memory_space=pltpu.HBM)] * 2,
        scratch_shapes=[dma((2,))],
    )(*[pltpu.with_memory_space_constraint(result, pltpu.VMEM) for result in results])


def solution(mesh):
    in_specs = (
        P(("row", "col"), None),
        P(("row", "col"), None),
        P(("row", "col"), None),
        P(),
        P("row", "col", None, None, None),
        P("row", "col", None, None),
        P("row", "col"),
    )
    out_specs = (P(("col", "row"), None), P())
    return jax.shard_map(local, mesh=mesh, in_specs=in_specs, out_specs=out_specs, check_vma=False)
```

```python
import functools

import jax
import jax.numpy as jnp
from jax import lax
from jax.experimental import pallas as pl
from jax.experimental.pallas import tpu as pltpu
from jax.sharding import PartitionSpec as P

MESH = pl.DeviceIdType.MESH
F32 = jnp.float32
BF16 = jnp.bfloat16

TILE = 128
SLOTS = 320
COLS = 32
HALF = 64
PAIRS = SLOTS // 2 + COLS // 2
LANES = 384
UNROLL = 88
CHUNKS = 4


def order_slots(coords, count):
    def total(condition, value, axis):
        return jnp.sum(jnp.where(condition, value, 0), axis=axis, keepdims=True)

    def iota(shape, axis):
        return lax.broadcasted_iota(jnp.int32, shape, axis)

    square = (SLOTS, SLOTS)
    down, across = iota(square, 0), iota(square, 1)
    live = iota((1, SLOTS), 1) < jnp.broadcast_to(count, (1, SLOTS))
    row = coords[0:1, :]
    key = jnp.where(live, coords[1:2, :], COLS)
    key_all = jnp.broadcast_to(key, square)
    key_down = total(down == across, key_all, 1)
    row_down = total(down == across, jnp.broadcast_to(row, square), 1)
    rank = total((key_down == key_all) & (across < down), 1, 1)

    member = key_down == iota((SLOTS, 128), 1)
    count_lane = total(member, 1, 0)
    count_down = total(jnp.broadcast_to(key, (COLS, SLOTS)) == iota((COLS, SLOTS), 0), 1, 1)
    padded_lane = (count_lane + 1) // 2 * 2
    padded_down = (count_down + 1) // 2 * 2
    low, high = iota((COLS, 128), 0), iota((COLS, 128), 1)
    start_lane = total(low < high, padded_down, 0)
    start_down = total(high < low, padded_lane, 1)

    place = jnp.where(key_down < COLS, total(member, start_lane, 1) + rank, -1)
    payload = iota((SLOTS, 1), 0) * 64 + row_down - COLS
    packed = COLS + total(place == iota((SLOTS, LANES), 1), payload, 0)

    pair = 2 * iota((COLS, LANES), 1)
    keep = 1 - total((start_down == pair) & (count_down > 0), 1, 0)
    last = jnp.where(count_lane > 0, (start_lane + padded_lane) // 2 - 1, PAIRS)
    return packed, keep, last


def kernel(
    out_grad, relu_mask, saved_agg, weight, tile_values, coords, count, input_grad, weight_grad,
    og, rm, sa, wt, tiles, xy, ct, meta_v, meta,
    agg0, agg1, run0, run1, xsend, xrecv, zsend, zrecv, own, term, w1, w1s, w2, w3,
    load_sem, tile_sem, first_recv, second_recv, gather_send,
    xs_sem, xr_sem, zs_sem, zr_sem, w_send, w_recv, near_sem,
):
    row, col = lax.axis_index("row"), lax.axis_index("col")
    z, core, x, y = row // 2, row % 2, col // 4, col % 4

    def at(xx, yy):
        return (row, xx % 4 * 4 + yy % 4)

    turn = 1 - 2 * core

    def up(d):
        return ((z + d + 8) % 8 * 2 + core, col)

    partner = (z * 2 + 1 - core, col)

    barrier = pltpu.get_barrier_semaphore()
    peers = [at(x + d, y) for d in (1, 2, 3)] + [at(x, y + d) for d in (1, 2, 3)] + [up(d) for d in (1, 2, 6, 7)] + [partner]
    for peer in peers:
        pl.semaphore_signal(barrier, inc=1, device_id=peer, device_id_type=MESH)

    loads = [
        pltpu.make_async_copy(src, dst, load_sem.at[i])
        for i, (src, dst) in enumerate(
            ((out_grad, og), (relu_mask, rm), (weight, wt), (saved_agg, sa), (coords, xy), (count, ct))
        )
    ]
    for load in loads:
        load.start()
    step = SLOTS // CHUNKS
    tile_loads = [
        pltpu.make_async_copy(
            tile_values.at[0, 0, pl.ds(i * step, step)], tiles.at[pl.ds(i * step, step)], tile_sem.at[i]
        )
        for i in range(CHUNKS)
    ]
    for load in tile_loads:
        load.start()

    aggs, runs = (agg0, agg1), (run0, run1)
    for agg in aggs:
        agg[COLS] = jnp.zeros((HALF, TILE), BF16)
    for run in runs:
        run[PAIRS] = jnp.zeros((HALF, TILE), F32)

    for load in loads[:3]:
        load.wait()
    pre = (og[...].astype(F32) * rm[...].astype(F32)).astype(BF16)
    mine = lax.dot_general(wt[...], pre, (((1,), (1,)), ((), ())), preferred_element_type=F32).astype(BF16)
    for h in range(2):
        for e in range(2):
            aggs[h][2 * col + e] = mine[h * HALF : (h + 1) * HALF, e * TILE : (e + 1) * TILE]

    loads[4].wait()
    loads[5].wait()
    packed, keep, last = order_slots(xy[...], ct[...])
    meta_v[...] = jnp.full((8, LANES), PAIRS, jnp.int32)
    meta_v[0:1, :] = packed
    meta_v[1:2, :] = keep
    meta_v[2:3, 0:128] = last
    to_scalar = pltpu.make_async_copy(meta_v, meta, load_sem.at[6])
    to_scalar.start()

    pl.semaphore_wait(barrier, len(peers))
    for d in (2, 6):
        pl.semaphore_signal(near_sem, inc=1, device_id=up(d), device_id_type=MESH)

    def toward(e, phase, d):
        return at(x + d, y) if (e + phase) % 2 == 0 else at(x, y + d)

    def piece(e, d):
        a, b = ((x - d) % 4, y) if e == 0 else (x, (y - d) % 4)
        return 2 * (a * 4 + b) + e

    def gather_copy(h, r, recv, target):
        block = aggs[h].at[r]
        return pltpu.make_async_remote_copy(
            src_ref=block, dst_ref=block, send_sem=gather_send.at[h], recv_sem=recv, device_id=target, device_id_type=MESH
        )

    def second(h, e, r):
        for d in (2, 1, 3):
            gather_copy(h, r, second_recv.at[h], toward(e, 1, d)).start()

    for h in range(2):
        for e in range(2):
            for d in (2, 1, 3):
                gather_copy(h, 2 * col + e, first_recv.at[h * 6 + e * 3 + d - 1], toward(e, 0, d)).start()
        for e in range(2):
            second(h, e, 2 * col + e)

    loads[3].wait()
    term[...] = lax.dot_general(sa[...], pre, (((0,), (0,)), ((), ())), preferred_element_type=F32)

    def rows(start, size):
        return pl.ds(pl.multiple_of(start, 8), size)

    def share(i, src, dst, target):
        return pltpu.make_async_remote_copy(
            src_ref=src, dst_ref=dst, send_sem=w_send.at[i], recv_sem=w_recv.at[i], device_id=target, device_id_type=MESH
        )

    def plain(ref, sem):
        return pltpu.make_async_copy(ref, ref, sem)

    def added(ref, n):
        value = ref[0]
        for i in range(1, n):
            value = value + ref[i]
        return value

    half_rows = rows(core * 64, 64)
    share(0, term.at[rows((1 - core) * 64, 64)], w1, partner).start()

    share(0, w1, w1, partner).wait_recv()
    w1s[...] = term[half_rows, :] + w1[...]
    w2[z] = w1s[rows(z * 8, 8), :]
    pl.semaphore_wait(near_sem, 2)
    for d in (4, 3, 5, 2, 6, 1, 7):
        share(1, w1s.at[rows((z + d) % 8 * 8, 8)], w2.at[z], up(d)).start()

    for h in range(2):
        for d in (1, 3, 2):
            for e in range(2):
                r = piece(e, d)
                gather_copy(h, r, first_recv.at[h * 6 + e * 3 + d - 1], toward(e, 0, d)).wait_recv()
                second(h, e, r)

    to_scalar.wait()
    for load in tile_loads:
        load.wait()

    def gathered(h):
        plain(aggs[h].at[pl.ds(0, 24)], second_recv.at[h]).wait()

    def products(h):
        agg, run = aggs[h], runs[h]

        def body(t, total):
            for u in range(UNROLL):
                q = t * UNROLL + u
                a, b = meta[0, 2 * q], meta[0, 2 * q + 1]
                left = jnp.concatenate([agg[a & 63], agg[b & 63]], axis=1)
                right = jnp.concatenate([tiles[a >> 6], tiles[b >> 6]], axis=0)
                total = total * meta[1, q].astype(F32) + jnp.dot(left, right, preferred_element_type=F32)
                run[q] = total
            return total

        lax.fori_loop(0, PAIRS // UNROLL, body, jnp.zeros((HALF, TILE), F32))

    def swap(h, far):
        part = pl.ds(5, 3) if far else pl.ds(0, 5)
        return pltpu.make_async_remote_copy(
            src_ref=xsend.at[h, part], dst_ref=xrecv.at[h, part], send_sem=xs_sem.at[h, int(far)],
            recv_sem=xr_sem.at[h, int(far)], device_id=partner, device_id_type=MESH,
        )

    def column(h, owner, k, e):
        return runs[h][meta[2, owner * 4 + k * 2 + e]]

    def scatter_swap(h):
        for far in (True, False):
            for slot in (6, 5, 7) if far else (0, 1, 3, 4, 2):
                for e in range(2):
                    xsend[h, slot, e] = column(h, (z + slot + 6) % 8, 1 - core, e).astype(BF16)
            swap(h, far).start()

    roles = (4, 3, -3, 1, -1, 2, -2)

    def scatter_copy(h, r):
        i, step = roles.index(r), {4: -2, 3: -1, -3: 1, 1: -1, -1: 1, 2: -2, -2: 2}[r]
        return pltpu.make_async_remote_copy(
            src_ref=zsend.at[h, i], dst_ref=zrecv.at[h, i], send_sem=zs_sem.at[h, i], recv_sem=zr_sem.at[h, i],
            device_id=up(turn * step), device_id_type=MESH,
        )

    def pair_sum(h, r, e):
        slot = (2 - turn * r + 8) % 8
        return column(h, (z - turn * r + 8) % 8, core, e) + xrecv[h, slot, e].astype(F32)

    def send_roles(h, some):
        for r in some:
            for e in range(2):
                zsend[h, roles.index(r), e] = pair_sum(h, r, e).astype(BF16)
            scatter_copy(h, r).start()

    def scatter_first(h):
        swap(h, True).wait_recv()
        send_roles(h, roles[:3])

    def scatter_near(h):
        swap(h, False).wait_recv()
        send_roles(h, roles[3:5])
        for i, r in enumerate((2, -2, 0)):
            for e in range(2):
                own[h, i, e] = pair_sum(h, r, e)

    def scatter_far(h):
        for r, sources in ((-2, (-3,)), (2, (4, 3))):
            for q in sources:
                scatter_copy(h, q).wait_recv()
            for e in range(2):
                value = own[h, 0 if r == 2 else 1, e]
                for q in sources:
                    value = value + zrecv[h, roles.index(q), e].astype(F32)
                zsend[h, roles.index(r), e] = value.astype(BF16)
            scatter_copy(h, r).start()

    def scattered(h):
        result = []
        for r in roles[3:]:
            scatter_copy(h, r).wait_recv()
        for e in range(2):
            value = own[h, 2, e]
            for i in range(3, 7):
                value = value + zrecv[h, i, e].astype(F32)
            result.append(value)
        return result

    gathered(0)
    plain(w2.at[pl.ds(0, 7)], w_recv.at[1]).wait()
    w3[col] = added(w2, 8)
    for a, b in ((2, 2), (1, 2), (3, 2), (2, 1), (2, 3), (0, 2), (2, 0), (1, 1), (1, 3), (3, 1), (3, 3), (0, 1), (0, 3), (1, 0), (3, 0)):
        share(2, w3.at[col], w3.at[col], at(x + a, y + b)).start()
    products(0)
    scatter_swap(0)
    scatter_first(0)
    scatter_near(0)
    gathered(1)
    products(1)
    scatter_swap(1)
    plain(w3.at[pl.ds(0, 15)], w_recv.at[2]).wait()
    mine_rows = rows(core * 64 + z * 8, 8)
    weight_grad[mine_rows, :] = added(w3, 16)
    for d in (4, 3, 5, 2, 6, 1, 7):
        share(4, weight_grad.at[mine_rows], weight_grad.at[mine_rows], up(d)).start()
    scatter_first(1)
    scatter_far(0)
    scatter_near(1)
    scatter_far(1)

    first_half = scattered(0)
    plain(weight_grad.at[pl.ds(0, 56)], w_recv.at[4]).wait()
    share(5, weight_grad.at[half_rows], weight_grad.at[half_rows], partner).start()
    second_half = scattered(1)
    for e in range(2):
        whole = jnp.concatenate([first_half[e], second_half[e]], axis=0)
        input_grad[e * TILE : (e + 1) * TILE, :] = whole.T.astype(BF16)

    plain(weight_grad.at[pl.ds(0, 64)], w_recv.at[5]).wait()
    for i, size in ((0, 64), (1, 56), (2, 120), (4, 56), (5, 64)):
        plain(term.at[pl.ds(0, size)], w_send.at[i]).wait()
    for h in range(2):
        plain(aggs[h].at[pl.ds(0, 30)], gather_send.at[h]).wait()
        for far in (True, False):
            swap(h, far).wait_send()
        for r in roles:
            scatter_copy(h, r).wait_send()


def write_out(input_grad, weight_grad, input_out, weight_out, sems):
    copies = [
        pltpu.make_async_copy(input_grad, input_out, sems.at[0]),
        pltpu.make_async_copy(weight_grad, weight_out, sems.at[1]),
    ]
    for copy in copies:
        copy.start()
    for copy in copies:
        copy.wait()


def local(out_grad, relu_mask, saved_agg, weight, tile_values, tile_coords, tile_count):
    nodes = out_grad.shape[0]
    vmem, dma = pltpu.VMEM, pltpu.SemaphoreType.DMA
    results = pl.pallas_call(
        kernel,
        out_shape=(
            pltpu.VMEM((nodes, TILE), BF16),
            pltpu.VMEM((TILE, TILE), F32),
        ),
        in_specs=[pl.BlockSpec(memory_space=pltpu.HBM)] * 7,
        out_specs=(pl.BlockSpec(memory_space=pltpu.VMEM), pl.BlockSpec(memory_space=pltpu.VMEM)),
        scratch_shapes=[
            vmem((nodes, TILE), BF16),
            vmem((nodes, TILE), BF16),
            vmem((nodes, TILE), BF16),
            vmem((TILE, TILE), BF16),
            vmem((SLOTS, TILE, TILE), BF16),
            vmem((2, SLOTS), jnp.int32),
            vmem((1, 1), jnp.int32),
            vmem((8, LANES), jnp.int32),
            pltpu.SMEM((8, LANES), jnp.int32),
            vmem((COLS + 1, HALF, TILE), BF16),
            vmem((COLS + 1, HALF, TILE), BF16),
            vmem((PAIRS + 1, HALF, TILE), F32),
            vmem((PAIRS + 1, HALF, TILE), F32),
            vmem((2, 8, 2, HALF, TILE), BF16),
            vmem((2, 8, 2, HALF, TILE), BF16),
            vmem((2, 7, 2, HALF, TILE), BF16),
            vmem((2, 7, 2, HALF, TILE), BF16),
            vmem((2, 3, 2, HALF, TILE), F32),
            vmem((TILE, TILE), F32),
            vmem((64, TILE), F32),
            vmem((64, TILE), F32),
            vmem((8, 8, TILE), F32),
            vmem((16, 8, TILE), F32),
            dma((7,)),
            dma((CHUNKS,)),
            dma((12,)),
            dma((2,)),
            dma((2,)),
            dma((2, 2)),
            dma((2, 2)),
            dma((2, 7)),
            dma((2, 7)),
            dma((6,)),
            dma((6,)),
            pltpu.SemaphoreType.REGULAR,
        ],
        compiler_params=pltpu.CompilerParams(
            collective_id=0, has_side_effects=True, vmem_limit_bytes=48 * 1024 * 1024
        ),
    )(*[
        pltpu.with_memory_space_constraint(array, pltpu.HBM)
        for array in (out_grad, relu_mask, saved_agg, weight, tile_values, tile_coords[0, 0].T)
    ], tile_count)
    return pl.pallas_call(
        write_out,
        out_shape=(pltpu.HBM((nodes, TILE), BF16), pltpu.HBM((TILE, TILE), F32)),
        in_specs=[pl.BlockSpec(memory_space=pltpu.VMEM)] * 2,
        out_specs=[pl.BlockSpec(memory_space=pltpu.HBM)] * 2,
        scratch_shapes=[dma((2,))],
    )(*[pltpu.with_memory_space_constraint(result, pltpu.VMEM) for result in results])


def solution(mesh):
    in_specs = (
        P(("row", "col"), None),
        P(("row", "col"), None),
        P(("row", "col"), None),
        P(),
        P("row", "col", None, None, None),
        P("row", "col", None, None),
        P("row", "col"),
    )
    out_specs = (P(("col", "row"), None), P())
    return jax.shard_map(local, mesh=mesh, in_specs=in_specs, out_specs=out_specs, check_vma=False)
```

```python
import functools

import jax
import jax.numpy as jnp
from jax import lax
from jax.experimental import pallas as pl
from jax.experimental.pallas import tpu as pltpu
from jax.sharding import PartitionSpec as P

MESH = pl.DeviceIdType.MESH
F32 = jnp.float32
BF16 = jnp.bfloat16

TILE = 128
SLOTS = 320
COLS = 32
HALF = 64
PAIRS = SLOTS // 2 + COLS // 2
LANES = 384
UNROLL = 88
CHUNKS = 4


def order_slots(coords, count):
    def total(condition, value, axis):
        return jnp.sum(jnp.where(condition, value, 0), axis=axis, keepdims=True)

    def iota(shape, axis):
        return lax.broadcasted_iota(jnp.int32, shape, axis)

    square = (SLOTS, SLOTS)
    down, across = iota(square, 0), iota(square, 1)
    live = iota((1, SLOTS), 1) < jnp.broadcast_to(count, (1, SLOTS))
    row = coords[0:1, :]
    key = jnp.where(live, coords[1:2, :], COLS)
    key_all = jnp.broadcast_to(key, square)
    key_down = total(down == across, key_all, 1)
    row_down = total(down == across, jnp.broadcast_to(row, square), 1)
    rank = total((key_down == key_all) & (across < down), 1, 1)

    member = key_down == iota((SLOTS, 128), 1)
    count_lane = total(member, 1, 0)
    count_down = total(jnp.broadcast_to(key, (COLS, SLOTS)) == iota((COLS, SLOTS), 0), 1, 1)
    padded_lane = (count_lane + 1) // 2 * 2
    padded_down = (count_down + 1) // 2 * 2
    low, high = iota((COLS, 128), 0), iota((COLS, 128), 1)
    start_lane = total(low < high, padded_down, 0)
    start_down = total(high < low, padded_lane, 1)

    place = jnp.where(key_down < COLS, total(member, start_lane, 1) + rank, -1)
    payload = iota((SLOTS, 1), 0) * 64 + row_down - COLS
    packed = COLS + total(place == iota((SLOTS, LANES), 1), payload, 0)

    pair = 2 * iota((COLS, LANES), 1)
    keep = 1 - total((start_down == pair) & (count_down > 0), 1, 0)
    last = jnp.where(count_lane > 0, (start_lane + padded_lane) // 2 - 1, PAIRS)
    return packed, keep, last


def kernel(
    out_grad, relu_mask, saved_agg, weight, tile_values, coords, count, input_grad, weight_grad,
    og, rm, sa, wt, tiles, xy, ct, meta_v, meta,
    agg0, agg1, run0, run1, xsend, xrecv, zsend, zrecv, own, term, w1, w1s, w2, w3,
    load_sem, tile_sem, first_recv, second_recv, gather_send,
    xs_sem, xr_sem, zs_sem, zr_sem, w_send, w_recv, near_sem,
):
    row, col = lax.axis_index("row"), lax.axis_index("col")
    z, core, x, y = row // 2, row % 2, col // 4, col % 4

    def at(xx, yy):
        return (row, xx % 4 * 4 + yy % 4)

    turn = 1 - 2 * core

    def up(d):
        return ((z + d + 8) % 8 * 2 + core, col)

    partner = (z * 2 + 1 - core, col)

    barrier = pltpu.get_barrier_semaphore()
    peers = [at(x + d, y) for d in (1, 2, 3)] + [at(x, y + d) for d in (1, 2, 3)] + [up(d) for d in (1, 2, 6, 7)] + [partner]
    for peer in peers:
        pl.semaphore_signal(barrier, inc=1, device_id=peer, device_id_type=MESH)

    loads = [
        pltpu.make_async_copy(src, dst, load_sem.at[i])
        for i, (src, dst) in enumerate(
            ((out_grad, og), (relu_mask, rm), (weight, wt), (saved_agg, sa), (coords, xy), (count, ct))
        )
    ]
    for load in loads:
        load.start()
    step = SLOTS // CHUNKS
    tile_loads = [
        pltpu.make_async_copy(
            tile_values.at[0, 0, pl.ds(i * step, step)], tiles.at[pl.ds(i * step, step)], tile_sem.at[i]
        )
        for i in range(CHUNKS)
    ]
    for load in tile_loads:
        load.start()

    aggs, runs = (agg0, agg1), (run0, run1)
    for agg in aggs:
        agg[COLS] = jnp.zeros((HALF, TILE), BF16)
    for run in runs:
        run[PAIRS] = jnp.zeros((HALF, TILE), F32)

    for load in loads[:3]:
        load.wait()
    pre = (og[...].astype(F32) * rm[...].astype(F32)).astype(BF16)
    mine = lax.dot_general(wt[...], pre, (((1,), (1,)), ((), ())), preferred_element_type=F32).astype(BF16)
    for h in range(2):
        for e in range(2):
            aggs[h][2 * col + e] = mine[h * HALF : (h + 1) * HALF, e * TILE : (e + 1) * TILE]

    loads[4].wait()
    loads[5].wait()
    packed, keep, last = order_slots(xy[...], ct[...])
    meta_v[...] = jnp.full((8, LANES), PAIRS, jnp.int32)
    meta_v[0:1, :] = packed
    meta_v[1:2, :] = keep
    meta_v[2:3, 0:128] = last
    to_scalar = pltpu.make_async_copy(meta_v, meta, load_sem.at[6])
    to_scalar.start()

    pl.semaphore_wait(barrier, len(peers))
    for d in (2, 6):
        pl.semaphore_signal(near_sem, inc=1, device_id=up(d), device_id_type=MESH)

    def toward(e, phase, d):
        return at(x + d, y) if (e + phase) % 2 == 0 else at(x, y + d)

    def piece(e, d):
        a, b = ((x - d) % 4, y) if e == 0 else (x, (y - d) % 4)
        return 2 * (a * 4 + b) + e

    def gather_copy(h, r, recv, target):
        block = aggs[h].at[r]
        return pltpu.make_async_remote_copy(
            src_ref=block, dst_ref=block, send_sem=gather_send.at[h], recv_sem=recv, device_id=target, device_id_type=MESH
        )

    def second(h, e, r):
        for d in (2, 1, 3):
            gather_copy(h, r, second_recv.at[h], toward(e, 1, d)).start()

    for h in range(2):
        for e in range(2):
            for d in (2, 1, 3):
                gather_copy(h, 2 * col + e, first_recv.at[h * 6 + e * 3 + d - 1], toward(e, 0, d)).start()
        for e in range(2):
            second(h, e, 2 * col + e)

    loads[3].wait()
    term[...] = lax.dot_general(sa[...], pre, (((0,), (0,)), ((), ())), preferred_element_type=F32)

    def rows(start, size):
        return pl.ds(pl.multiple_of(start, 8), size)

    def share(i, src, dst, target):
        return pltpu.make_async_remote_copy(
            src_ref=src, dst_ref=dst, send_sem=w_send.at[i], recv_sem=w_recv.at[i], device_id=target, device_id_type=MESH
        )

    def plain(ref, sem):
        return pltpu.make_async_copy(ref, ref, sem)

    def added(ref, n):
        value = ref[0]
        for i in range(1, n):
            value = value + ref[i]
        return value

    half_rows = rows(core * 64, 64)
    share(0, term.at[rows((1 - core) * 64, 64)], w1, partner).start()

    share(0, w1, w1, partner).wait_recv()
    w1s[...] = term[half_rows, :] + w1[...]
    w2[z] = w1s[rows(z * 8, 8), :]
    pl.semaphore_wait(near_sem, 2)
    for d in (4, 3, 5, 2, 6, 1, 7):
        share(1, w1s.at[rows((z + d) % 8 * 8, 8)], w2.at[z], up(d)).start()

    for h in range(2):
        for d in (1, 3, 2):
            for e in range(2):
                r = piece(e, d)
                gather_copy(h, r, first_recv.at[h * 6 + e * 3 + d - 1], toward(e, 0, d)).wait_recv()
                second(h, e, r)

    to_scalar.wait()
    for load in tile_loads:
        load.wait()

    def gathered(h):
        plain(aggs[h].at[pl.ds(0, 24)], second_recv.at[h]).wait()

    def products(h):
        agg, run = aggs[h], runs[h]

        def body(t, total):
            for u in range(UNROLL):
                q = t * UNROLL + u
                a, b = meta[0, 2 * q], meta[0, 2 * q + 1]
                left = jnp.concatenate([agg[a & 63], agg[b & 63]], axis=1)
                right = jnp.concatenate([tiles[a >> 6], tiles[b >> 6]], axis=0)
                total = total * meta[1, q].astype(F32) + jnp.dot(left, right, preferred_element_type=F32)
                run[q] = total
            return total

        lax.fori_loop(0, PAIRS // UNROLL, body, jnp.zeros((HALF, TILE), F32))

    def swap(h, far):
        part = pl.ds(5, 3) if far else pl.ds(0, 5)
        return pltpu.make_async_remote_copy(
            src_ref=xsend.at[h, part], dst_ref=xrecv.at[h, part], send_sem=xs_sem.at[h, int(far)],
            recv_sem=xr_sem.at[h, int(far)], device_id=partner, device_id_type=MESH,
        )

    def column(h, owner, k, e):
        return runs[h][meta[2, owner * 4 + k * 2 + e]]

    def scatter_swap(h):
        for far in (True, False):
            for slot in (6, 5, 7) if far else (0, 1, 3, 4, 2):
                for e in range(2):
                    xsend[h, slot, e] = column(h, (z + slot + 6) % 8, 1 - core, e).astype(BF16)
            swap(h, far).start()

    roles = (4, 3, -3, 1, -1, 2, -2)

    def scatter_copy(h, r):
        i, step = roles.index(r), {4: -2, 3: -1, -3: 1, 1: -1, -1: 1, 2: -2, -2: 2}[r]
        return pltpu.make_async_remote_copy(
            src_ref=zsend.at[h, i], dst_ref=zrecv.at[h, i], send_sem=zs_sem.at[h, i], recv_sem=zr_sem.at[h, i],
            device_id=up(turn * step), device_id_type=MESH,
        )

    def pair_sum(h, r, e):
        slot = (2 - turn * r + 8) % 8
        return column(h, (z - turn * r + 8) % 8, core, e) + xrecv[h, slot, e].astype(F32)

    def send_roles(h, some):
        for r in some:
            for e in range(2):
                zsend[h, roles.index(r), e] = pair_sum(h, r, e).astype(BF16)
            scatter_copy(h, r).start()

    def scatter_first(h):
        swap(h, True).wait_recv()
        send_roles(h, roles[:3])

    def scatter_near(h):
        swap(h, False).wait_recv()
        send_roles(h, roles[3:5])
        for i, r in enumerate((2, -2, 0)):
            for e in range(2):
                own[h, i, e] = pair_sum(h, r, e)

    def scatter_far(h):
        for r, sources in ((-2, (-3,)), (2, (4, 3))):
            for q in sources:
                scatter_copy(h, q).wait_recv()
            for e in range(2):
                value = own[h, 0 if r == 2 else 1, e]
                for q in sources:
                    value = value + zrecv[h, roles.index(q), e].astype(F32)
                zsend[h, roles.index(r), e] = value.astype(BF16)
            scatter_copy(h, r).start()

    def scattered(h):
        result = []
        for r in roles[3:]:
            scatter_copy(h, r).wait_recv()
        for e in range(2):
            value = own[h, 2, e]
            for i in range(3, 7):
                value = value + zrecv[h, i, e].astype(F32)
            result.append(value)
        return result

    gathered(0)
    plain(w2.at[pl.ds(0, 7)], w_recv.at[1]).wait()
    w3[col] = added(w2, 8)
    for a, b in ((2, 2), (1, 2), (3, 2), (2, 1), (2, 3), (0, 2), (2, 0), (1, 1), (1, 3), (3, 1), (3, 3), (0, 1), (0, 3), (1, 0), (3, 0)):
        share(2, w3.at[col], w3.at[col], at(x + a, y + b)).start()
    products(0)
    scatter_swap(0)
    scatter_first(0)
    scatter_near(0)
    gathered(1)
    products(1)
    scatter_swap(1)
    plain(w3.at[pl.ds(0, 15)], w_recv.at[2]).wait()
    mine_rows = rows(core * 64 + z * 8, 8)
    weight_grad[mine_rows, :] = added(w3, 16)
    for d in (4, 3, 5, 2, 6, 1, 7):
        share(4, weight_grad.at[mine_rows], weight_grad.at[mine_rows], up(d)).start()
    scatter_first(1)
    scatter_far(0)
    scatter_near(1)
    scatter_far(1)

    def finish(h):
        for e, value in enumerate(scattered(h)):
            input_grad[e * TILE : (e + 1) * TILE, h * HALF : (h + 1) * HALF] = value.T.astype(BF16)

    finish(0)
    plain(weight_grad.at[pl.ds(0, 56)], w_recv.at[4]).wait()
    share(5, weight_grad.at[half_rows], weight_grad.at[half_rows], partner).start()
    finish(1)

    plain(weight_grad.at[pl.ds(0, 64)], w_recv.at[5]).wait()
    for i, size in ((0, 64), (1, 56), (2, 120), (4, 56), (5, 64)):
        plain(term.at[pl.ds(0, size)], w_send.at[i]).wait()
    for h in range(2):
        plain(aggs[h].at[pl.ds(0, 30)], gather_send.at[h]).wait()
        for far in (True, False):
            swap(h, far).wait_send()
        for r in roles:
            scatter_copy(h, r).wait_send()


def write_out(input_grad, weight_grad, input_out, weight_out, sems):
    copies = [
        pltpu.make_async_copy(input_grad, input_out, sems.at[0]),
        pltpu.make_async_copy(weight_grad, weight_out, sems.at[1]),
    ]
    for copy in copies:
        copy.start()
    for copy in copies:
        copy.wait()


def local(out_grad, relu_mask, saved_agg, weight, tile_values, tile_coords, tile_count):
    nodes = out_grad.shape[0]
    vmem, dma = pltpu.VMEM, pltpu.SemaphoreType.DMA
    results = pl.pallas_call(
        kernel,
        out_shape=(
            pltpu.VMEM((nodes, TILE), BF16),
            pltpu.VMEM((TILE, TILE), F32),
        ),
        in_specs=[pl.BlockSpec(memory_space=pltpu.HBM)] * 7,
        out_specs=(pl.BlockSpec(memory_space=pltpu.VMEM), pl.BlockSpec(memory_space=pltpu.VMEM)),
        scratch_shapes=[
            vmem((nodes, TILE), BF16),
            vmem((nodes, TILE), BF16),
            vmem((nodes, TILE), BF16),
            vmem((TILE, TILE), BF16),
            vmem((SLOTS, TILE, TILE), BF16),
            vmem((2, SLOTS), jnp.int32),
            vmem((1, 1), jnp.int32),
            vmem((8, LANES), jnp.int32),
            pltpu.SMEM((8, LANES), jnp.int32),
            vmem((COLS + 1, HALF, TILE), BF16),
            vmem((COLS + 1, HALF, TILE), BF16),
            vmem((PAIRS + 1, HALF, TILE), F32),
            vmem((PAIRS + 1, HALF, TILE), F32),
            vmem((2, 8, 2, HALF, TILE), BF16),
            vmem((2, 8, 2, HALF, TILE), BF16),
            vmem((2, 7, 2, HALF, TILE), BF16),
            vmem((2, 7, 2, HALF, TILE), BF16),
            vmem((2, 3, 2, HALF, TILE), F32),
            vmem((TILE, TILE), F32),
            vmem((64, TILE), F32),
            vmem((64, TILE), F32),
            vmem((8, 8, TILE), F32),
            vmem((16, 8, TILE), F32),
            dma((7,)),
            dma((CHUNKS,)),
            dma((12,)),
            dma((2,)),
            dma((2,)),
            dma((2, 2)),
            dma((2, 2)),
            dma((2, 7)),
            dma((2, 7)),
            dma((6,)),
            dma((6,)),
            pltpu.SemaphoreType.REGULAR,
        ],
        compiler_params=pltpu.CompilerParams(
            collective_id=0, has_side_effects=True, vmem_limit_bytes=48 * 1024 * 1024
        ),
    )(*[
        pltpu.with_memory_space_constraint(array, pltpu.HBM)
        for array in (out_grad, relu_mask, saved_agg, weight, tile_values, tile_coords[0, 0].T)
    ], tile_count)
    return pl.pallas_call(
        write_out,
        out_shape=(pltpu.HBM((nodes, TILE), BF16), pltpu.HBM((TILE, TILE), F32)),
        in_specs=[pl.BlockSpec(memory_space=pltpu.VMEM)] * 2,
        out_specs=[pl.BlockSpec(memory_space=pltpu.HBM)] * 2,
        scratch_shapes=[dma((2,))],
    )(*[pltpu.with_memory_space_constraint(result, pltpu.VMEM) for result in results])


def solution(mesh):
    in_specs = (
        P(("row", "col"), None),
        P(("row", "col"), None),
        P(("row", "col"), None),
        P(),
        P("row", "col", None, None, None),
        P("row", "col", None, None),
        P("row", "col"),
    )
    out_specs = (P(("col", "row"), None), P())
    return jax.shard_map(local, mesh=mesh, in_specs=in_specs, out_specs=out_specs, check_vma=False)
```
